256 devices in a mesh: view: 8 (over z_lo, x), tile: 32 (over y, z_hi, core).
Axes of the slice: x: 4, y: 4, z: 8 (z_hi: 4, z_lo: 2; z = z_hi * 2 + z_lo), core: 2. Of those that a mesh axis runs over, the one named last changes fastest.
Arguments:
- estimate: float32 [16, 1024, 1024], P(None, 'tile', 'view'), may hold values from 0.5 to 2
- measured: bfloat16 [8, 16, 1024, 1024], P('view', None, 'tile'), may hold values from 0.05 to 12
- psf_z: float32 [8, 65], P('view'), may hold values from 0.05 to 1
- psf_xy: float32 [8, 2, 9], P('view'), may hold values from 0.1 to 1
- offsets: int32 [8, 2], P('view'), may hold values from -4 to 4, as said below
- coverage: int32 [8, 32], P('view', 'tile'), may hold values from 0 to 1, as said below
Outputs:
- restored: float32 [16, 1024, 1024], P(None, 'tile', 'view')
The draws below stay inside these ranges and needn't reach their ends.
Inputs may be any that keep to these rules, and one draw needn't show every extreme that they name: offsets[v, 0] shifts view v along rows and offsets[v, 1] along columns; some view has a row offset of 4 and some view a column offset of -4. coverage[v, t] is 1 where view v images rows t * 32 to (t + 1) * 32 - 1, else 0; every tile is imaged by at least one view.
All inputs are finite; a program needn't handle non-finite values.
Results may differ from the reference program's by a relative error of at most 0.0006.
Values may be sent and summed in bfloat16 or wider, within the bound.
A program may use at most 64 MiB of HBM per device.

```python
import math
import jax
import jax.numpy as jnp
from jax import lax

NZ = 16
TY = 32
NXT = 1024
RZ = 32
SHIFT = 4
ITERS = 2
VIEWS = 8
TILES = 32
NY = 1024
KZ = 65
KXY = 9


def draw_estimate(key, part):
    first_key = jax.random.fold_in(jax.random.fold_in(key, 53), 0)
    values = jnp.exp(jax.random.uniform(first_key, (NZ, NY, NXT), jnp.float32, math.log(0.5), math.log(2.0)))
    return values.astype(jnp.float32)


def draw_measured(key, part):
    keys = jax.random.split(jax.random.fold_in(key, 37), 6)
    two_pi = 2.0 * math.pi
    wave_z = jax.random.uniform(keys[0], (4,), jnp.float32, 12.0, 64.0)
    wave_y = jax.random.uniform(keys[1], (4,), jnp.float32, 16.0, 256.0)
    wave_x = jax.random.uniform(keys[2], (4,), jnp.float32, 16.0, 256.0)
    phases = jax.random.uniform(keys[3], (4, 3), jnp.float32, 0.0, two_pi)
    plane_pos = jnp.arange(NZ, dtype=jnp.float32)
    row_pos = jnp.arange(NY, dtype=jnp.float32)
    col_pos = jnp.arange(NXT, dtype=jnp.float32)
    smooth = jnp.zeros((NZ, NY, NXT), jnp.float32)
    for term in range(4):
        along_z = jnp.cos(two_pi * plane_pos / wave_z[term] + phases[term, 0])
        along_y = jnp.cos(two_pi * row_pos / wave_y[term] + phases[term, 1])
        along_x = jnp.cos(two_pi * col_pos / wave_x[term] + phases[term, 2])
        smooth = smooth + along_z[:, None, None] * along_y[None, :, None] * along_x[None, None, :]
    brightness = jnp.exp(jax.random.uniform(keys[4], (VIEWS, 1, 1, 1), jnp.float32, math.log(0.7), math.log(1.4)))
    truth = jnp.exp(0.3 * smooth)
    rough = jnp.exp(jax.random.uniform(keys[5], (VIEWS, NZ, NY, NXT), jnp.float32, math.log(0.5), math.log(2.0)))
    return (brightness * truth[None] * rough).astype(jnp.bfloat16)


def draw_offsets(key, part):
    first_key, second_key, third_key = jax.random.split(jax.random.fold_in(key, 11), 3)
    values = jax.random.randint(first_key, (VIEWS, 2), -SHIFT, SHIFT + 1, dtype=jnp.int32)
    top_view = jax.random.randint(second_key, (), 0, VIEWS, dtype=jnp.int32)
    low_view = jax.random.randint(third_key, (), 0, VIEWS, dtype=jnp.int32)
    values = values.at[top_view, 0].set(SHIFT)
    values = values.at[low_view, 1].set(-SHIFT)
    return values


def draw_coverage(key, part):
    first_key, second_key, third_key = jax.random.split(jax.random.fold_in(key, 23), 3)
    levels = jax.random.randint(first_key, (VIEWS, 1), 1, 4, dtype=jnp.int32)
    coin_draws = jax.random.randint(second_key, (VIEWS, TILES), 0, 4, dtype=jnp.int32)
    chosen = jax.random.randint(third_key, (TILES,), 0, VIEWS, dtype=jnp.int32)
    view_ids = jnp.arange(VIEWS, dtype=jnp.int32)[:, None]
    random_part = (coin_draws < levels).astype(jnp.int32)
    forced_part = (view_ids == chosen[None, :]).astype(jnp.int32)
    return jnp.maximum(random_part, forced_part)


def shard_levels(key, shape, cuts, least, largest):
    factor_of = 1.0
    for dim, blocks in cuts:
        steps = jax.random.uniform(jax.random.fold_in(jax.random.fold_in(key, 6), dim), (blocks,), jnp.float32, least / len(cuts), largest / len(cuts))
        factor_of = factor_of * jnp.repeat(jnp.exp(steps), shape[dim] // blocks).reshape((-1,) + (1,) * (len(shape) - 1 - dim))
    return factor_of


def setup_inputs(seed: int = 0) -> dict:
    splits = jax.random.split(jax.random.key(seed), 7)
    return {
        "estimate": draw_estimate(jax.random.fold_in(splits[6], 71), 0),
        "measured": draw_measured(jax.random.fold_in(splits[6], 71), 0),
        "psf_z": jnp.clip(jnp.exp(math.log(1.0) - 2.9957323 * jax.random.uniform(splits[2], (VIEWS, KZ), jnp.float32) ** shard_levels(splits[2], (VIEWS, KZ), ((0, 8),), -0.2, 0.2)), 0.05, 1.0),
        "psf_xy": jnp.clip(jnp.exp(math.log(1.0) - 2.3025851 * jax.random.uniform(splits[3], (VIEWS, 2, KXY), jnp.float32) ** shard_levels(splits[3], (VIEWS, 2, KXY), ((0, 8),), -0.2, 0.2)), 0.1, 1.0),
        "offsets": draw_offsets(jax.random.fold_in(splits[6], 71), 0),
        "coverage": draw_coverage(jax.random.fold_in(splits[6], 71), 0),
    }


EXACT_MATMUL = lax.Precision.HIGHEST


def band_matrix(kernel, n_in, n_out, lead_offset):
    count_taps = kernel.shape[-1]
    rows_in = jnp.arange(n_in, dtype=jnp.int32)[:, None]
    rows_out = jnp.arange(n_out, dtype=jnp.int32)[None, :]
    tap_ids = jnp.arange(count_taps, dtype=jnp.int32)[:, None, None]
    selector = ((rows_in - rows_out + lead_offset)[None] == tap_ids).astype(jnp.float32)
    return jnp.tensordot(kernel, selector, axes=1, precision=EXACT_MATMUL)


def place_kernel(kernel, shift_value):
    count_taps = kernel.shape[0]
    positions = jnp.arange(count_taps + 2 * SHIFT, dtype=jnp.int32)[None, :]
    tap_ids = jnp.arange(count_taps, dtype=jnp.int32)[:, None]
    selector = (positions == tap_ids + SHIFT + shift_value.astype(jnp.int32)).astype(jnp.float32)
    return jnp.dot(kernel, selector, precision=EXACT_MATMUL)


def shifted_sum(object_volume, kernel, axis):
    count_taps = kernel.shape[0]
    margin = (count_taps - 1) // 2
    size_axis = object_volume.shape[axis]
    pad_widths = [(0, 0), (0, 0), (0, 0)]
    pad_widths[axis] = (margin, margin)
    padded = jnp.pad(object_volume, pad_widths)
    result = jnp.zeros_like(object_volume)
    for tap_index in range(count_taps):
        result = result + kernel[tap_index] * lax.slice_in_dim(padded, tap_index, tap_index + size_axis, axis=axis)
    return result


def reference(estimate, measured, psf_z, psf_xy, offsets, coverage):
    current = estimate
    view_count = jnp.repeat(jnp.sum(coverage, axis=0), TY).astype(jnp.float32)
    for iteration in range(ITERS):
        log_total = jnp.zeros_like(current)
        for view_index in range(VIEWS):
            z_kernel = psf_z[view_index] / jnp.sum(psf_z[view_index])
            y_kernel = psf_xy[view_index, 0] / jnp.sum(psf_xy[view_index, 0])
            x_kernel = psf_xy[view_index, 1] / jnp.sum(psf_xy[view_index, 1])
            depth_banded = band_matrix(z_kernel, NZ, NZ, RZ)
            y_taps = place_kernel(y_kernel, offsets[view_index, 0])
            x_taps = place_kernel(x_kernel, offsets[view_index, 1])
            blurred = jnp.einsum("ab,ayx->byx", depth_banded, current, precision=EXACT_MATMUL)
            blurred = shifted_sum(blurred, y_taps, 1)
            blurred = shifted_sum(blurred, x_taps, 2)
            measurement_ratios = measured[view_index].astype(jnp.float32) / blurred
            updated_estimate = jnp.einsum("ab,byx->ayx", depth_banded, measurement_ratios, precision=EXACT_MATMUL)
            updated_estimate = shifted_sum(updated_estimate, jnp.flip(y_taps), 1)
            updated_estimate = shifted_sum(updated_estimate, jnp.flip(x_taps), 2)
            covered = jnp.repeat(coverage[view_index], TY).astype(jnp.float32)
            log_total = log_total + covered[None, :, None] * jnp.log(updated_estimate)
        current = current * jnp.exp(log_total / view_count[None, :, None])
    return current
```

```python
import functools

import jax
import jax.numpy as jnp
from jax import lax
from jax.experimental import pallas as pl
from jax.experimental.pallas import tpu as pltpu
from jax.sharding import PartitionSpec as P

MESH = pl.DeviceIdType.MESH
F32, BF16 = jnp.float32, jnp.bfloat16
SHIFT, ITERS = 4, 2
NZ, TY, BX, NV, NT = 16, 32, 128, 8, 32
KZ, KXY = 65, 9
EXACT = lax.Precision.HIGHEST


def lanes(shape):
    return lax.broadcasted_iota(jnp.int32, shape, len(shape) - 1)


def toeplitz(row, count):
    x = jnp.broadcast_to(row, (count, row.shape[-1]))
    r = lax.broadcasted_iota(jnp.int32, x.shape, 0)
    bit = 1
    while bit < count:
        x = jnp.where((r & bit) != 0, pltpu.roll(x, bit, 1), x)
        bit *= 2
    return x


def kernel(
    est, meas, pz, pxy, offs, cov, out,
    mbuf, pb, fld, hr, hl, sr, sl, mm, mq, mu, md, sq, su, sd,
    rz, ry, az, ay, wf, wb, xf, xb, bl, rt, acc, cur,
    loc, ps, pr, fs, fr, ms, mr,
):
    v, t = lax.axis_index("view"), lax.axis_index("tile")
    has_up, has_down = t > 0, t < NT - 1
    has_left, has_right = v > 0, v < NV - 1

    def remote(src, dst, send, recv, dv, dt):
        return pltpu.make_async_remote_copy(
            src_ref=src, dst_ref=dst, send_sem=send, recv_sem=recv, device_id=(dv, dt), device_id_type=MESH
        )

    own_cols = pl.ds(pl.multiple_of(v * BX, BX), BX)
    get_all = pltpu.make_async_copy(meas.at[0], mbuf, loc.at[0])
    get_own = pltpu.make_async_copy(meas.at[0, :, :, own_cols], mm.at[v], loc.at[1])
    get_all.start()
    get_own.start()

    barrier = pltpu.get_barrier_semaphore()
    tiles = (t, lax.rem(t + 1, NT), lax.rem(t + NT - 1, NT))
    for s in range(NV):
        for k, dt in enumerate(tiles):
            if s or k:
                pl.semaphore_signal(barrier, inc=1, device_id=(lax.rem(v + s, NV), dt), device_id_type=MESH)

    lane1 = lanes((1, BX))
    zero1 = jnp.zeros((1, BX), F32)

    def taps(values, places):
        row = zero1
        for value, place in zip(values, places):
            row = jnp.where(lane1 == place, value, row)
        return row

    z_taps = [pz[0, i] for i in range(KZ)]
    y_taps = [pxy[0, 0, i] for i in range(KXY)]
    x_taps = [pxy[0, 1, i] for i in range(KXY)]
    oy, ox = offs[0, 0], offs[0, 1]

    def normal(values):
        return jnp.full((1, BX), functools.reduce(lambda a, b: a + b, values), F32)

    zn, yn, xn = normal(z_taps), normal(y_taps), normal(x_taps)
    rows = [
        taps(z_taps, range(KZ)) / zn,
        taps(z_taps, [KZ - 1 - i for i in range(KZ)]) / zn,
        taps(y_taps, [i + SHIFT + oy for i in range(KXY)]) / yn,
        taps(y_taps, [16 - (i + SHIFT + oy) for i in range(KXY)]) / yn,
        taps(x_taps, [4 - i - ox for i in range(KXY)]) / xn,
        taps(x_taps, [132 - i - ox for i in range(KXY)]) / xn,
        taps(x_taps, [i - 4 + ox for i in range(KXY)]) / xn,
        taps(x_taps, [i + 124 + ox for i in range(KXY)]) / xn,
        jnp.full((1, BX), cov[0, 0].astype(F32)),
    ]
    for i, row in enumerate(rows):
        pb[v, i : i + 1, :] = row
    pb[v, len(rows) :, :] = jnp.zeros((16 - len(rows), BX), F32)

    pl.semaphore_wait(barrier, 3 * NV - 1)

    for s in range(1, NV):
        d = lax.rem(v + s, NV)
        remote(pb.at[v], pb.at[v], ps.at[d], pr.at[v], d, t).start()

    plane_lane = lanes((TY, BX))
    wide_lane = lanes((2 * TY, BX))

    def field_copies(it):
        f = fld.at[it]
        up, down, left, right = t - 1, t + 1, v - 1, v + 1
        top, low = pl.ds(0, 16), pl.ds(16, 16)
        main = pl.ds(0, BX)
        specs = [
            (has_up, has_down, f.at[:, pl.ds(16, 16), main], f.at[:, pl.ds(48, 16), main], v, up),
            (has_down, has_up, f.at[:, pl.ds(32, 16), main], f.at[:, pl.ds(0, 16), main], v, down),
        ]
        for ok_to, ok_from, s, h, dv in ((has_left, has_right, sr, hr, left), (has_right, has_left, sl, hl, right)):
            specs += [
                (ok_to, ok_from, s.at[it], h.at[it, :, pl.ds(16, 32)], dv, t),
                (ok_to & has_up, ok_from & has_down, s.at[it, :, top], h.at[it, :, pl.ds(48, 16)], dv, up),
                (ok_to & has_down, ok_from & has_up, s.at[it, :, low], h.at[it, :, pl.ds(0, 16)], dv, down),
            ]
        return [
            (ok_to, ok_from, dst, remote(src, dst, fs.at[it, i], fr.at[it, i], dv, dt))
            for i, (ok_to, ok_from, src, dst, dv, dt) in enumerate(specs)
        ]

    def send_field(it, source):
        for z in range(NZ):
            fld[it, z, 16:48, 0:BX] = source[z].astype(BF16)
        copies = field_copies(it)
        for ok_to, _, _, copy in copies[:2]:
            pl.when(ok_to)(copy.start)
        for q in range(2):
            head = jnp.zeros((TY, BX), F32)
            tail = jnp.zeros((TY, BX), F32)
            for k in range(8):
                rolled = source[8 * q + k]
                if k:
                    rolled = pltpu.roll(rolled, 16 * k, 1)
                head = jnp.where(plane_lane // 16 == k, rolled, head)
                tail = jnp.where(plane_lane // 16 == (k + 7) % 8, rolled, tail)
            sr[it, q] = head.astype(BF16)
            sl[it, q] = tail.astype(BF16)
        for ok_to, _, _, copy in copies[2:]:
            pl.when(ok_to)(copy.start)

    def receive_field(it):
        for _, ok_from, dst, copy in field_copies(it):
            pl.when(ok_from)(copy.wait_recv)

            @pl.when(jnp.logical_not(ok_from))
            def _():
                dst[...] = jnp.zeros(dst.shape, BF16)

        for q in range(2):
            right = hr[it, q].astype(F32)
            left = hl[it, q].astype(F32)
            for k in range(8):
                both = jnp.where(wide_lane // 16 == k, right, left)
                if k:
                    both = pltpu.roll(both, BX - 16 * k, 1)
                both = jnp.where((wide_lane < 16) | (wide_lane >= 112), both, 0.0)
                fld[it, 8 * q + k, :, BX:] = both.astype(BF16)

    send_field(0, est)

    get_all.wait()
    for s in range(1, NV):
        d = lax.rem(v + s, NV)
        cols = pl.ds(pl.multiple_of(d * BX, BX), BX)
        remote(mbuf.at[:, :, cols], mm.at[v], ms.at[0, d], mr.at[0, v], d, t).start()

    def pack_measured(s, carry):
        d = lax.rem(v + s, NV)
        here = pl.ds(pl.multiple_of(d * BX, BX), BX)
        after = pl.ds(pl.multiple_of(jnp.minimum(d + 1, NV - 1) * BX, BX), BX)
        before = pl.ds(pl.multiple_of(jnp.maximum(d - 1, 0) * BX, BX), BX)
        take_after = (plane_lane < 8) & (d < NV - 1)
        take_before = (plane_lane >= 120) & (d > 0)
        corners = []
        for q in range(2):
            packed = jnp.zeros((TY, BX), F32)
            for k in range(8):
                z = 8 * q + k
                edge = jnp.where(
                    take_after, mbuf[z, :, after].astype(F32),
                    jnp.where(take_before, mbuf[z, :, before].astype(F32), 0.0),
                )
                packed = packed + (pltpu.roll(edge, 16 * k, 1) if k else edge)
            sq[d, q] = packed.astype(BF16)
            corners.append(packed)
        for p in range(NZ // 2):
            a = mbuf[2 * p, :, here].astype(F32)
            b = mbuf[2 * p + 1, :, here].astype(F32)
            sd[d, p] = jnp.concatenate([a[0:8], b[0:8]], axis=0).astype(BF16)
            su[d, p] = jnp.concatenate([a[24:32], b[24:32]], axis=0).astype(BF16)
        sd[d, 8] = jnp.concatenate([corners[0][0:8], corners[1][0:8]], axis=0).astype(BF16)
        su[d, 8] = jnp.concatenate([corners[0][24:32], corners[1][24:32]], axis=0).astype(BF16)

        @pl.when(d != v)
        def _():
            remote(sq.at[d], mq.at[v], ms.at[1, d], mr.at[1, v], d, t).start()

        @pl.when(has_down)
        def _():
            remote(su.at[d], mu.at[v], ms.at[2, d], mr.at[2, v], d, t + 1).start()

        @pl.when(has_up)
        def _():
            remote(sd.at[d], md.at[v], ms.at[3, d], mr.at[3, v], d, t - 1).start()

        return carry

    lax.fori_loop(0, NV, pack_measured, 0)
    mq[v] = sq[v]

    for s in range(1, NV):
        u = lax.rem(v + s, NV)
        remote(pb.at[u], pb.at[u], ps.at[u], pr.at[u], u, t).wait_recv()

    def small_bands(u, carry):
        z16 = pl.ds(pl.multiple_of(u * 16, 16), 16)
        for half in range(2):
            rz[half, z16, :] = toeplitz(pb[u, half : half + 1, :], 16)
            ry[half, z16, :] = toeplitz(pb[u, 2 + half : 3 + half, :], 16)
        for source, target in ((4, xf), (6, xb)):
            row = jnp.concatenate([pb[u, source : source + 1, :], pb[u, source + 1 : source + 2, :]], axis=1)
            base = toeplitz(row, 16)
            width = target.shape[-1]
            for g in range(16):
                part = (pltpu.roll(base, 16 * g, 1) if g else base)[:, :width]
                high = part.astype(BF16)
                target[0, u, 16 * g : 16 * g + 16, :] = high
                target[1, u, 16 * g : 16 * g + 16, :] = (part - high.astype(F32)).astype(BF16)
        return carry

    lax.fori_loop(0, NV, small_bands, 0)
    m = lax.broadcasted_iota(jnp.int32, (BX, 512), 0)
    n = lanes((BX, 512))
    spread_z = (m == n // 32 + 32).astype(F32)
    spread_y = (m == n % 32).astype(F32)
    for half in range(2):
        az[half] = jnp.dot(rz[half], spread_z, precision=EXACT, preferred_element_type=F32)
        ay[half] = jnp.dot(ry[half], spread_y, precision=EXACT, preferred_element_type=F32)

    def depth_rows(u, carry):
        z16 = pl.ds(pl.multiple_of(u * 16, 16), 16)
        for half, target in enumerate((wf, wb)):
            a = az[half, z16, :]
            y = ay[half, z16, :]
            for z in range(NZ):
                target[u, 16 * z : 16 * z + 16, :] = (a[z : z + 1] * y).astype(BF16)
        return carry

    lax.fori_loop(0, NV, depth_rows, 0)

    def forward(it):
        receive_field(it)

        def view(u, carry):
            for c in range(3):
                chunk = fld[it, :, 16 * c : 16 * c + 32, :].reshape(512, 256)
                zy = jnp.dot(wf[u], chunk, preferred_element_type=F32).astype(BF16)
                full = jnp.dot(zy, xf[0, u], preferred_element_type=F32)
                full = full + jnp.dot(zy, xf[1, u], preferred_element_type=F32)
                bl[u, :, 16 * c : 16 * c + 16, :] = full.reshape(NZ, 16, 256)
            return carry

        lax.fori_loop(0, NV, view, 0)

    ext_lane = lanes((48, BX))

    def wait_measured(u):
        @pl.when(u != v)
        def _():
            remote(mbuf.at[:, :, pl.ds(0, BX)], mm.at[u], ms.at[0, u], mr.at[0, u], u, t).wait_recv()
            remote(sq.at[u], mq.at[u], ms.at[1, u], mr.at[1, u], u, t).wait_recv()

        @pl.when(has_up)
        def _():
            remote(su.at[u], mu.at[u], ms.at[2, u], mr.at[2, u], u, t).wait_recv()

        @pl.when(has_down)
        def _():
            remote(sd.at[u], md.at[u], ms.at[3, u], mr.at[3, u], u, t).wait_recv()

    @pl.when(jnp.logical_not(has_up))
    def _():
        mu[...] = jnp.zeros(mu.shape, BF16)

    @pl.when(jnp.logical_not(has_down))
    def _():
        md[...] = jnp.zeros(md.shape, BF16)

    def ratio(values, blurred):
        return jnp.where(values > 0, values / blurred, 0.0).astype(BF16)

    def backward(first):
        acc[...] = jnp.zeros(acc.shape, F32)

        def view(s, carry):
            u = lax.rem(v + s, NV)
            if first:
                wait_measured(u)
            cu, cd = mu[u, 8].astype(F32), md[u, 8].astype(F32)
            for q in range(2):
                rows8 = slice(8 * q, 8 * q + 8)
                edge = jnp.concatenate([cu[rows8], mq[u, q].astype(F32), cd[rows8]], axis=0)
                for k in range(8):
                    z = 8 * q + k
                    side = pltpu.roll(edge, BX - 16 * k, 1) if k else edge
                    side = jnp.where((ext_lane < 8) | (ext_lane >= 120), side, 0.0)
                    rt[z, :, BX:] = ratio(side, bl[u, z, :, BX:])
                    r = slice(8 * (z % 2), 8 * (z % 2) + 8)
                    main = jnp.concatenate(
                        [mu[u, z // 2].astype(F32)[r], mm[u, z].astype(F32), md[u, z // 2].astype(F32)[r]], axis=0
                    )
                    rt[z, :, :BX] = ratio(main, bl[u, z, :, :BX])
            weight = pb[u, 8:9, :]
            for c in range(2):
                chunk = rt[:, 16 * c : 16 * c + 32, :].reshape(512, 256)
                zy = jnp.dot(wb[u], chunk, preferred_element_type=F32)
                high = zy.astype(BF16)
                low = (zy - high.astype(F32)).astype(BF16)
                back = jnp.dot(high, xb[0, u], preferred_element_type=F32)
                back = back + jnp.dot(low, xb[0, u], preferred_element_type=F32)
                back = back + jnp.dot(high, xb[1, u], preferred_element_type=F32)
                acc[:, 16 * c : 16 * c + 16, :] += (weight * jnp.log(back)).reshape(NZ, 16, BX)
            return carry

        lax.fori_loop(0, NV, view, 0)

    count = pb[0, 8:9, :]
    for u in range(1, NV):
        count = count + pb[u, 8:9, :]

    get_own.wait()
    forward(0)
    backward(True)
    for z in range(NZ):
        cur[z] = est[z] * jnp.exp(acc[z] / count)
    send_field(1, cur)
    forward(1)
    backward(False)
    for z in range(NZ):
        out[z] = cur[z] * jnp.exp(acc[z] / count)

    for it in range(ITERS):
        for ok_to, _, _, copy in field_copies(it):
            pl.when(ok_to)(copy.wait_send)

    def drain(s, carry):
        d = lax.rem(v + s, NV)

        @pl.when(d != v)
        def _():
            remote(pb.at[v], pb.at[v], ps.at[d], pr.at[d], d, t).wait_send()
            remote(mbuf.at[:, :, pl.ds(0, BX)], mm.at[v], ms.at[0, d], mr.at[0, d], d, t).wait_send()
            remote(sq.at[d], mq.at[v], ms.at[1, d], mr.at[1, d], d, t).wait_send()

        @pl.when(has_down)
        def _():
            remote(su.at[d], mu.at[v], ms.at[2, d], mr.at[2, d], d, t).wait_send()

        @pl.when(has_up)
        def _():
            remote(sd.at[d], md.at[v], ms.at[3, d], mr.at[3, d], d, t).wait_send()

        return carry

    lax.fori_loop(0, NV, drain, 0)


def body(estimate, measured, psf_z, psf_xy, offsets, coverage):
    vmem = pl.BlockSpec(memory_space=pltpu.VMEM)
    smem = pl.BlockSpec(memory_space=pltpu.SMEM)
    scratch = [
        ((NZ, TY, NV * BX), BF16), ((NV, 16, BX), F32),
        ((2, NZ, 64, 256), BF16), ((2, 2, 64, BX), BF16), ((2, 2, 64, BX), BF16),
        ((2, 2, TY, BX), BF16), ((2, 2, TY, BX), BF16),
        ((NV, NZ, TY, BX), BF16), ((NV, 2, TY, BX), BF16), ((NV, 9, 16, BX), BF16), ((NV, 9, 16, BX), BF16),
        ((NV, 2, TY, BX), BF16), ((NV, 9, 16, BX), BF16), ((NV, 9, 16, BX), BF16),
        ((2, 128, BX), F32), ((2, 128, BX), F32), ((2, 128, 512), F32), ((2, 128, 512), F32),
        ((NV, 256, 512), BF16), ((NV, 256, 512), BF16), ((2, NV, 256, 256), BF16), ((2, NV, 256, BX), BF16),
        ((NV, NZ, 48, 256), F32), ((NZ, 48, 256), BF16), ((NZ, TY, BX), F32), ((NZ, TY, BX), F32),
    ]
    dma = pltpu.SemaphoreType.DMA
    return pl.pallas_call(
        kernel,
        out_shape=jax.ShapeDtypeStruct(estimate.shape, F32),
        in_specs=[vmem, pl.BlockSpec(memory_space=pl.ANY), smem, smem, smem, smem],
        out_specs=vmem,
        scratch_shapes=[pltpu.VMEM(s, d) for s, d in scratch]
        + [dma((2,)), dma((NV,)), dma((NV,)), dma((2, 8)), dma((2, 8)), dma((4, NV)), dma((4, NV))],
        compiler_params=pltpu.CompilerParams(
            collective_id=0, has_side_effects=True, vmem_limit_bytes=48 * 1024 * 1024
        ),
    )(estimate, measured, psf_z, psf_xy, offsets, coverage)


def solution(mesh):
    placed = (
        P(None, "tile", "view"),
        P("view", None, "tile", None),
        P("view", None),
        P("view", None, None),
        P("view", None),
        P("view", "tile"),
    )
    return jax.shard_map(
        body, mesh=mesh, in_specs=placed, out_specs=P(None, "tile", "view"), check_vma=False
    )
```

```python
import functools

import jax
import jax.numpy as jnp
from jax import lax
from jax.experimental import pallas as pl
from jax.experimental.pallas import tpu as pltpu
from jax.sharding import PartitionSpec as P

MESH = pl.DeviceIdType.MESH
F32, BF16 = jnp.float32, jnp.bfloat16
SHIFT, ITERS = 4, 2
NZ, TY, BX, NV, NT = 16, 32, 128, 8, 32
KZ, KXY = 65, 9
EXACT = lax.Precision.HIGHEST


def lanes(shape):
    return lax.broadcasted_iota(jnp.int32, shape, len(shape) - 1)


def toeplitz(row, count):
    x = jnp.broadcast_to(row, (count, row.shape[-1]))
    r = lax.broadcasted_iota(jnp.int32, x.shape, 0)
    bit = 1
    while bit < count:
        x = jnp.where((r & bit) != 0, pltpu.roll(x, bit, 1), x)
        bit *= 2
    return x


def kernel(
    est_hbm, meas, pz_hbm, pxy_hbm, offs_hbm, cov_hbm, out,
    est, pz, pxy, offs, cov,
    mbuf, pb, fld, hr, hl, sr, sl, mm, mq, mu, md, sq, su, sd,
    rz, ry, az, ay, wf, wb, xf, xb, bl, mext, rt, acc, cur,
    loc, ps, pr, fs, fr, ms, mr,
):
    v, t = lax.axis_index("view"), lax.axis_index("tile")
    has_up, has_down = t > 0, t < NT - 1
    has_left, has_right = v > 0, v < NV - 1

    def remote(src, dst, send, recv, dv, dt):
        return pltpu.make_async_remote_copy(
            src_ref=src, dst_ref=dst, send_sem=send, recv_sem=recv, device_id=(dv, dt), device_id_type=MESH
        )

    own_cols = pl.ds(pl.multiple_of(v * BX, BX), BX)
    get_all = pltpu.make_async_copy(meas.at[0], mbuf, loc.at[0])
    get_own = pltpu.make_async_copy(meas.at[0, :, :, own_cols], mm.at[v], loc.at[1])
    small = [
        pltpu.make_async_copy(src, dst, loc.at[2 + i])
        for i, (src, dst) in enumerate(
            ((pz_hbm, pz), (pxy_hbm, pxy), (offs_hbm, offs), (cov_hbm, cov), (est_hbm, est))
        )
    ]
    for copy in small:
        copy.start()
    get_all.start()
    get_own.start()

    barrier = pltpu.get_barrier_semaphore()
    up_tile, down_tile = lax.rem(t + NT - 1, NT), lax.rem(t + 1, NT)
    partners = [(lax.rem(v + s, NV), t) for s in range(1, NV)]
    partners += [(lax.rem(v + s, NV), dt) for s in (0, 1, NV - 1) for dt in (up_tile, down_tile)]
    for partner in partners:
        pl.semaphore_signal(barrier, inc=1, device_id=partner, device_id_type=MESH)
    for copy in small[:4]:
        copy.wait()

    lane1 = lanes((1, BX))
    zero1 = jnp.zeros((1, BX), F32)

    def taps(values, places):
        row = zero1
        for value, place in zip(values, places):
            row = jnp.where(lane1 == place, value, row)
        return row

    z_taps = [pz[0, i] for i in range(KZ)]
    y_taps = [pxy[0, 0, i] for i in range(KXY)]
    x_taps = [pxy[0, 1, i] for i in range(KXY)]
    oy, ox = offs[0, 0], offs[0, 1]

    def normal(values):
        return jnp.full((1, BX), functools.reduce(lambda a, b: a + b, values), F32)

    zn, yn, xn = normal(z_taps), normal(y_taps), normal(x_taps)
    rows = [
        taps(z_taps, range(KZ)) / zn,
        taps(z_taps, [KZ - 1 - i for i in range(KZ)]) / zn,
        taps(y_taps, [i + SHIFT + oy for i in range(KXY)]) / yn,
        taps(y_taps, [16 - (i + SHIFT + oy) for i in range(KXY)]) / yn,
        taps(x_taps, [4 - i - ox for i in range(KXY)]) / xn,
        taps(x_taps, [132 - i - ox for i in range(KXY)]) / xn,
        taps(x_taps, [i - 4 + ox for i in range(KXY)]) / xn,
        taps(x_taps, [i + 124 + ox for i in range(KXY)]) / xn,
        jnp.full((1, BX), cov[0, 0].astype(F32)),
    ]
    for i, row in enumerate(rows):
        pb[v, i : i + 1, :] = row
    pb[v, len(rows) :, :] = jnp.zeros((16 - len(rows), BX), F32)

    plane_lane = lanes((TY, BX))
    wide_lane = lanes((2 * TY, BX))

    def field_copies(it):
        f = fld.at[it]
        up, down, left, right = t - 1, t + 1, v - 1, v + 1
        top, low = pl.ds(0, 16), pl.ds(16, 16)
        main = pl.ds(0, BX)
        specs = [
            (has_up, has_down, f.at[:, pl.ds(16, 16), main], f.at[:, pl.ds(48, 16), main], v, up),
            (has_down, has_up, f.at[:, pl.ds(32, 16), main], f.at[:, pl.ds(0, 16), main], v, down),
        ]
        for ok_to, ok_from, s, h, dv in ((has_left, has_right, sr, hr, left), (has_right, has_left, sl, hl, right)):
            specs += [
                (ok_to, ok_from, s.at[it], h.at[it, :, pl.ds(16, 32)], dv, t),
                (ok_to & has_up, ok_from & has_down, s.at[it, :, top], h.at[it, :, pl.ds(48, 16)], dv, up),
                (ok_to & has_down, ok_from & has_up, s.at[it, :, low], h.at[it, :, pl.ds(0, 16)], dv, down),
            ]
        return [
            (ok_to, ok_from, dst, remote(src, dst, fs.at[it, i], fr.at[it, i], dv, dt))
            for i, (ok_to, ok_from, src, dst, dv, dt) in enumerate(specs)
        ]

    def pack_field(it, source):
        for z in range(NZ):
            fld[it, z, 16:48, 0:BX] = source[z].astype(BF16)
        for q in range(2):
            head = jnp.zeros((TY, BX), F32)
            tail = jnp.zeros((TY, BX), F32)
            for k in range(8):
                rolled = source[8 * q + k]
                if k:
                    rolled = pltpu.roll(rolled, 16 * k, 1)
                head = jnp.where(plane_lane // 16 == k, rolled, head)
                tail = jnp.where(plane_lane // 16 == (k + 7) % 8, rolled, tail)
            sr[it, q] = head.astype(BF16)
            sl[it, q] = tail.astype(BF16)

    def send_field(it):
        for ok_to, _, _, copy in field_copies(it):
            pl.when(ok_to)(copy.start)

    def receive_field(it):
        for _, ok_from, dst, copy in field_copies(it):
            pl.when(ok_from)(copy.wait_recv)

            @pl.when(jnp.logical_not(ok_from))
            def _():
                dst[...] = jnp.zeros(dst.shape, BF16)

        for q in range(2):
            right = hr[it, q].astype(F32)
            left = hl[it, q].astype(F32)
            for k in range(8):
                both = jnp.where(wide_lane // 16 == k, right, left)
                if k:
                    both = pltpu.roll(both, BX - 16 * k, 1)
                both = jnp.where((wide_lane < 16) | (wide_lane >= 112), both, 0.0)
                fld[it, 8 * q + k, :, BX:] = both.astype(BF16)

    small[4].wait()
    pack_field(0, est)
    get_all.wait()

    def pack_columns(d, carry):
        after = pl.ds(pl.multiple_of(jnp.minimum(d + 1, NV - 1) * BX, BX), BX)
        before = pl.ds(pl.multiple_of(jnp.maximum(d - 1, 0) * BX, BX), BX)
        take_after = (plane_lane < 8) & (d < NV - 1)
        take_before = (plane_lane >= 120) & (d > 0)
        for q in range(2):
            packed = jnp.zeros((TY, BX), F32)
            for k in range(8):
                z = 8 * q + k
                edge = jnp.where(
                    take_after, mbuf[z, :, after].astype(F32),
                    jnp.where(take_before, mbuf[z, :, before].astype(F32), 0.0),
                )
                packed = packed + (pltpu.roll(edge, 16 * k, 1) if k else edge)
            sq[d, q] = packed.astype(BF16)
        return carry

    lax.fori_loop(0, NV, pack_columns, 0)
    mq[v] = sq[v]

    pl.semaphore_wait(barrier, len(partners))
    for s in range(1, NV):
        d = lax.rem(v + s, NV)
        remote(pb.at[v], pb.at[v], ps.at[d], pr.at[v], d, t).start()
    send_field(0)
    for s in range(1, NV):
        d = lax.rem(v + s, NV)
        cols = pl.ds(pl.multiple_of(d * BX, BX), BX)
        remote(mbuf.at[:, :, cols], mm.at[v], ms.at[0, d], mr.at[0, v], d, t).start()
        remote(sq.at[d], mq.at[v], ms.at[1, d], mr.at[1, v], d, t).start()

    for s in range(1, NV):
        u = lax.rem(v + s, NV)
        remote(pb.at[u], pb.at[u], ps.at[u], pr.at[u], u, t).wait_recv()

    def small_bands(u, carry):
        z16 = pl.ds(pl.multiple_of(u * 16, 16), 16)
        for half in range(2):
            rz[half, z16, :] = toeplitz(pb[u, half : half + 1, :], 16)
            ry[half, z16, :] = toeplitz(pb[u, 2 + half : 3 + half, :], 16)
        for source, target in ((4, xf), (6, xb)):
            row = jnp.concatenate([pb[u, source : source + 1, :], pb[u, source + 1 : source + 2, :]], axis=1)
            base = toeplitz(row, 16)
            width = target.shape[-1]
            for g in range(16):
                part = (pltpu.roll(base, 16 * g, 1) if g else base)[:, :width]
                target[u, 16 * g : 16 * g + 16, :] = part.astype(BF16)
        return carry

    lax.fori_loop(0, NV, small_bands, 0)
    m = lax.broadcasted_iota(jnp.int32, (BX, 512), 0)
    n = lanes((BX, 512))
    spread_z = (m == n // 32 + 32).astype(F32)
    spread_y = (m == n % 32).astype(F32)
    for half in range(2):
        az[half] = jnp.dot(rz[half], spread_z, precision=EXACT, preferred_element_type=F32)
        ay[half] = jnp.dot(ry[half], spread_y, precision=EXACT, preferred_element_type=F32)

    def depth_rows(u, carry):
        z16 = pl.ds(pl.multiple_of(u * 16, 16), 16)
        for half, target in enumerate((wf, wb)):
            a = az[half, z16, :]
            y = ay[half, z16, :]
            for z in range(NZ):
                target[u, 16 * z : 16 * z + 16, :] = (a[z : z + 1] * y).astype(BF16)
        return carry

    lax.fori_loop(0, NV, depth_rows, 0)

    def blur(it, u):
        parts = []
        for c in range(3):
            chunk = fld[it, :, 16 * c : 16 * c + 32, :].reshape(512, 256)
            parts.append(jnp.dot(wf[u], chunk, preferred_element_type=F32).astype(BF16))
        return jnp.dot(jnp.concatenate(parts, axis=0), xf[u], preferred_element_type=F32)

    def relay_copies(u):
        return (
            (has_down, has_up, remote(su.at[u], mu.at[u], ms.at[2, u], mr.at[2, u], v, t + 1)),
            (has_up, has_down, remote(sd.at[u], md.at[u], ms.at[3, u], mr.at[3, u], v, t - 1)),
        )

    def relay(u):
        @pl.when(u != v)
        def _():
            remote(mbuf.at[:, :, pl.ds(0, BX)], mm.at[u], ms.at[0, u], mr.at[0, u], u, t).wait_recv()
            remote(sq.at[u], mq.at[u], ms.at[1, u], mr.at[1, u], u, t).wait_recv()

        for p in range(9):
            if p < 8:
                a, b = mm[u, 2 * p].astype(F32), mm[u, 2 * p + 1].astype(F32)
            else:
                a, b = mq[u, 0].astype(F32), mq[u, 1].astype(F32)
            sd[u, p] = jnp.concatenate([a[0:8], b[0:8]], axis=0).astype(BF16)
            su[u, p] = jnp.concatenate([a[24:32], b[24:32]], axis=0).astype(BF16)
        for ok_to, _, copy in relay_copies(u):
            pl.when(ok_to)(copy.start)

    ext_lane = lanes((48, BX))

    @pl.when(jnp.logical_not(has_up))
    def _():
        mu[...] = jnp.zeros(mu.shape, BF16)

    @pl.when(jnp.logical_not(has_down))
    def _():
        md[...] = jnp.zeros(md.shape, BF16)

    def ratio(values, blurred):
        return jnp.where(values > 0, values / blurred, 0.0).astype(BF16)

    def assemble(u):
        cu, cd = mu[u, 8].astype(F32), md[u, 8].astype(F32)
        for q in range(2):
            rows8 = slice(8 * q, 8 * q + 8)
            edge = jnp.concatenate([cu[rows8], mq[u, q].astype(F32), cd[rows8]], axis=0)
            for k in range(8):
                z = 8 * q + k
                side = pltpu.roll(edge, BX - 16 * k, 1) if k else edge
                side = jnp.where((ext_lane < 8) | (ext_lane >= 120), side, 0.0)
                mext[u, z, :, BX:] = side.astype(BF16)
                rt[z, :, BX:] = ratio(side, bl[u, z, :, BX:])
                r = slice(8 * (z % 2), 8 * (z % 2) + 8)
                main = jnp.concatenate(
                    [mu[u, z // 2].astype(F32)[r], mm[u, z].astype(F32), md[u, z // 2].astype(F32)[r]], axis=0
                )
                mext[u, z, :, :BX] = main.astype(BF16)
                rt[z, :, :BX] = ratio(main, bl[u, z, :, :BX])

    def correct(u, ratios):
        weight = pb[u, 8:9, :]
        rows = jnp.dot(ratios.reshape(768, 256), xb[u], preferred_element_type=F32).astype(BF16)
        rows = rows.reshape(NZ, 48, BX)
        chunks = jnp.concatenate([rows[:, 0:32].reshape(512, BX), rows[:, 16:48].reshape(512, BX)], axis=1)
        back = jnp.dot(wb[u], chunks, preferred_element_type=F32)
        for c in range(2):
            log_back = weight * jnp.log(back[:, BX * c : BX * c + BX])
            acc[:, 16 * c : 16 * c + 16, :] += log_back.reshape(NZ, 16, BX)

    count = pb[0, 8:9, :]
    for u in range(1, NV):
        count = count + pb[u, 8:9, :]

    get_own.wait()
    receive_field(0)
    acc[...] = jnp.zeros(acc.shape, F32)

    def source_view(s):
        return lax.rem(v + NV - s, NV)

    def first_forward(s, carry):
        u = source_view(s)
        full = blur(0, u)
        for c in range(3):
            bl[u, :, 16 * c : 16 * c + 16, :] = full[256 * c : 256 * c + 256].reshape(NZ, 16, 256)
        pl.when(s >= 4)(lambda: relay(source_view(s - 4)))
        return carry

    lax.fori_loop(0, NV, first_forward, 0)

    def first_backward(s, carry):
        u = source_view(s)
        pl.when(s < 4)(lambda: relay(source_view(s + 4)))
        for _, ok_from, copy in relay_copies(u):
            pl.when(ok_from)(copy.wait_recv)
        assemble(u)
        correct(u, rt[...])
        return carry

    lax.fori_loop(0, NV, first_backward, 0)
    for z in range(NZ):
        cur[z] = est[z] * jnp.exp(acc[z] / count)
    pack_field(1, cur)
    send_field(1)
    receive_field(1)
    acc[...] = jnp.zeros(acc.shape, F32)

    def second(u, carry):
        full = blur(1, u)
        for c in range(3):
            part = full[256 * c : 256 * c + 256].reshape(NZ, 16, 256)
            rt[:, 16 * c : 16 * c + 16, :] = ratio(mext[u, :, 16 * c : 16 * c + 16, :].astype(F32), part)
        correct(u, rt[...])
        return carry

    lax.fori_loop(0, NV, second, 0)
    for z in range(NZ):
        out[z] = cur[z] * jnp.exp(acc[z] / count)

    for it in range(ITERS):
        for ok_to, _, _, copy in field_copies(it):
            pl.when(ok_to)(copy.wait_send)

    def drain(s, carry):
        d = lax.rem(v + s, NV)

        @pl.when(d != v)
        def _():
            remote(pb.at[v], pb.at[v], ps.at[d], pr.at[d], d, t).wait_send()
            remote(mbuf.at[:, :, pl.ds(0, BX)], mm.at[v], ms.at[0, d], mr.at[0, d], d, t).wait_send()
            remote(sq.at[d], mq.at[v], ms.at[1, d], mr.at[1, d], d, t).wait_send()

        for ok_to, _, copy in relay_copies(d):
            pl.when(ok_to)(copy.wait_send)
        return carry

    lax.fori_loop(0, NV, drain, 0)


def body(estimate, measured, psf_z, psf_xy, offsets, coverage):
    scratch = [
        ((NZ, TY, NV * BX), BF16), ((NV, 16, BX), F32),
        ((2, NZ, 64, 256), BF16), ((2, 2, 64, BX), BF16), ((2, 2, 64, BX), BF16),
        ((2, 2, TY, BX), BF16), ((2, 2, TY, BX), BF16),
        ((NV, NZ, TY, BX), BF16), ((NV, 2, TY, BX), BF16), ((NV, 9, 16, BX), BF16), ((NV, 9, 16, BX), BF16),
        ((NV, 2, TY, BX), BF16), ((NV, 9, 16, BX), BF16), ((NV, 9, 16, BX), BF16),
        ((2, 128, BX), F32), ((2, 128, BX), F32), ((2, 128, 512), F32), ((2, 128, 512), F32),
        ((NV, 256, 512), BF16), ((NV, 256, 512), BF16), ((NV, 256, 256), BF16), ((NV, 256, BX), BF16),
        ((NV, NZ, 48, 256), F32), ((NV, NZ, 48, 256), BF16), ((NZ, 48, 256), BF16), ((NZ, TY, BX), F32), ((NZ, TY, BX), F32),
    ]
    dma = pltpu.SemaphoreType.DMA
    return pl.pallas_call(
        kernel,
        out_shape=jax.ShapeDtypeStruct(estimate.shape, F32),
        in_specs=[pl.BlockSpec(memory_space=pl.ANY)] * 6,
        out_specs=pl.BlockSpec(memory_space=pltpu.VMEM),
        scratch_shapes=[
            pltpu.VMEM((NZ, TY, BX), F32),
            pltpu.SMEM((1, KZ), F32),
            pltpu.SMEM((1, 2, KXY), F32),
            pltpu.SMEM((1, 2), jnp.int32),
            pltpu.SMEM((1, 1), jnp.int32),
        ]
        + [pltpu.VMEM(s, d) for s, d in scratch]
        + [dma((7,)), dma((NV,)), dma((NV,)), dma((2, 8)), dma((2, 8)), dma((4, NV)), dma((4, NV))],
        compiler_params=pltpu.CompilerParams(
            collective_id=0, has_side_effects=True, vmem_limit_bytes=48 * 1024 * 1024
        ),
    )(estimate, measured, psf_z, psf_xy, offsets, coverage)


def solution(mesh):
    placed = (
        P(None, "tile", "view"),
        P("view", None, "tile", None),
        P("view", None),
        P("view", None, None),
        P("view", None),
        P("view", "tile"),
    )
    return jax.shard_map(
        body, mesh=mesh, in_specs=placed, out_specs=P(None, "tile", "view"), check_vma=False
    )
```

```python
import functools

import jax
import jax.numpy as jnp
from jax import lax
from jax.experimental import pallas as pl
from jax.experimental.pallas import tpu as pltpu
from jax.sharding import PartitionSpec as P

MESH = pl.DeviceIdType.MESH
F32, BF16 = jnp.float32, jnp.bfloat16
SHIFT, ITERS = 4, 2
NZ, TY, BX, NV, NT = 16, 32, 128, 8, 32
KZ, KXY = 65, 9
EXACT = lax.Precision.HIGHEST


def lanes(shape):
    return lax.broadcasted_iota(jnp.int32, shape, len(shape) - 1)


def toeplitz(row, count):
    x = jnp.broadcast_to(row, (count, row.shape[-1]))
    r = lax.broadcasted_iota(jnp.int32, x.shape, 0)
    bit = 1
    while bit < count:
        x = jnp.where((r & bit) != 0, pltpu.roll(x, bit, 1), x)
        bit *= 2
    return x


def kernel(
    est_hbm, meas, pz_hbm, pxy_hbm, offs_hbm, cov_hbm, out,
    est, pz, pxy, offs, cov,
    mbuf, pb, fld, hr, hl, sr, sl, mm, mq, mu, md, sq, su, sd,
    rz, ry, az, ay, wf, wb, xf, xb, bl, mext, rt, acc, cur,
    loc, ps, pr, fs, fr, ms, mr,
):
    v, t = lax.axis_index("view"), lax.axis_index("tile")
    has_up, has_down = t > 0, t < NT - 1
    has_left, has_right = v > 0, v < NV - 1

    def remote(src, dst, send, recv, dv, dt):
        return pltpu.make_async_remote_copy(
            src_ref=src, dst_ref=dst, send_sem=send, recv_sem=recv, device_id=(dv, dt), device_id_type=MESH
        )

    half, spot = v // 4, lax.rem(v, 4)

    def target_view(s):
        return lax.rem(half + s // 4, 2) * 4 + lax.rem(spot + s, 4)

    def source_view(s):
        return lax.rem(half + s // 4, 2) * 4 + lax.rem(spot + 8 - s, 4)

    own_cols = pl.ds(pl.multiple_of(v * BX, BX), BX)
    get_all = pltpu.make_async_copy(meas.at[0], mbuf, loc.at[0])
    get_own = pltpu.make_async_copy(meas.at[0, :, :, own_cols], mm.at[v], loc.at[1])
    small = [
        pltpu.make_async_copy(src, dst, loc.at[2 + i])
        for i, (src, dst) in enumerate(
            ((pz_hbm, pz), (pxy_hbm, pxy), (offs_hbm, offs), (cov_hbm, cov), (est_hbm, est))
        )
    ]
    for copy in small:
        copy.start()
    get_all.start()
    get_own.start()

    barrier = pltpu.get_barrier_semaphore()
    up_tile, down_tile = lax.rem(t + NT - 1, NT), lax.rem(t + 1, NT)
    partners = [(lax.rem(v + s, NV), t) for s in range(1, NV)]
    partners += [(lax.rem(v + s, NV), dt) for s in (0, 1, NV - 1) for dt in (up_tile, down_tile)]
    for partner in partners:
        pl.semaphore_signal(barrier, inc=1, device_id=partner, device_id_type=MESH)
    for copy in small[:4]:
        copy.wait()

    lane1 = lanes((1, BX))
    zero1 = jnp.zeros((1, BX), F32)

    def taps(values, places):
        row = zero1
        for value, place in zip(values, places):
            row = jnp.where(lane1 == place, value, row)
        return row

    z_taps = [pz[0, i] for i in range(KZ)]
    y_taps = [pxy[0, 0, i] for i in range(KXY)]
    x_taps = [pxy[0, 1, i] for i in range(KXY)]
    oy, ox = offs[0, 0], offs[0, 1]

    def normal(values):
        return jnp.full((1, BX), functools.reduce(lambda a, b: a + b, values), F32)

    zn, yn, xn = normal(z_taps), normal(y_taps), normal(x_taps)
    rows = [
        taps(z_taps, range(KZ)) / zn,
        taps(z_taps, [KZ - 1 - i for i in range(KZ)]) / zn,
        taps(y_taps, [i + SHIFT + oy for i in range(KXY)]) / yn,
        taps(y_taps, [16 - (i + SHIFT + oy) for i in range(KXY)]) / yn,
        taps(x_taps, [4 - i - ox for i in range(KXY)]) / xn,
        taps(x_taps, [132 - i - ox for i in range(KXY)]) / xn,
        taps(x_taps, [i - 4 + ox for i in range(KXY)]) / xn,
        taps(x_taps, [i + 124 + ox for i in range(KXY)]) / xn,
        jnp.full((1, BX), cov[0, 0].astype(F32)),
    ]
    for i, row in enumerate(rows):
        pb[v, i : i + 1, :] = row
    pb[v, len(rows) :, :] = jnp.zeros((16 - len(rows), BX), F32)

    plane_lane = lanes((TY, BX))
    wide_lane = lanes((2 * TY, BX))

    def field_copies(it):
        f = fld.at[it]
        up, down, left, right = t - 1, t + 1, v - 1, v + 1
        top, low = pl.ds(0, 16), pl.ds(16, 16)
        main = pl.ds(0, BX)
        specs = [
            (has_up, has_down, f.at[:, pl.ds(16, 16), main], f.at[:, pl.ds(48, 16), main], v, up),
            (has_down, has_up, f.at[:, pl.ds(32, 16), main], f.at[:, pl.ds(0, 16), main], v, down),
        ]
        for ok_to, ok_from, s, h, dv in ((has_left, has_right, sr, hr, left), (has_right, has_left, sl, hl, right)):
            specs += [
                (ok_to, ok_from, s.at[it], h.at[it, :, pl.ds(16, 32)], dv, t),
                (ok_to & has_up, ok_from & has_down, s.at[it, :, top], h.at[it, :, pl.ds(48, 16)], dv, up),
                (ok_to & has_down, ok_from & has_up, s.at[it, :, low], h.at[it, :, pl.ds(0, 16)], dv, down),
            ]
        return [
            (ok_to, ok_from, dst, remote(src, dst, fs.at[it, i], fr.at[it, i], dv, dt))
            for i, (ok_to, ok_from, src, dst, dv, dt) in enumerate(specs)
        ]

    def pack_field(it, source):
        for z in range(NZ):
            fld[it, z, 16:48, 0:BX] = source[z].astype(BF16)
        for q in range(2):
            head = jnp.zeros((TY, BX), F32)
            tail = jnp.zeros((TY, BX), F32)
            for k in range(8):
                rolled = source[8 * q + k]
                if k:
                    rolled = pltpu.roll(rolled, 16 * k, 1)
                head = jnp.where(plane_lane // 16 == k, rolled, head)
                tail = jnp.where(plane_lane // 16 == (k + 7) % 8, rolled, tail)
            sr[it, q] = head.astype(BF16)
            sl[it, q] = tail.astype(BF16)

    def send_field(it):
        for ok_to, _, _, copy in field_copies(it):
            pl.when(ok_to)(copy.start)

    def receive_field(it):
        for _, ok_from, dst, copy in field_copies(it):
            pl.when(ok_from)(copy.wait_recv)

            @pl.when(jnp.logical_not(ok_from))
            def _():
                dst[...] = jnp.zeros(dst.shape, BF16)

        for q in range(2):
            right = hr[it, q].astype(F32)
            left = hl[it, q].astype(F32)
            for k in range(8):
                both = jnp.where(wide_lane // 16 == k, right, left)
                if k:
                    both = pltpu.roll(both, BX - 16 * k, 1)
                both = jnp.where((wide_lane < 16) | (wide_lane >= 112), both, 0.0)
                fld[it, 8 * q + k, :, BX:] = both.astype(BF16)

    small[4].wait()
    pack_field(0, est)
    get_all.wait()

    pl.semaphore_wait(barrier, len(partners))
    for s in range(1, NV):
        d = target_view(s)
        remote(pb.at[v], pb.at[v], ps.at[d], pr.at[v], d, t).start()
    send_field(0)
    for s in range(1, NV):
        d = target_view(s)
        cols = pl.ds(pl.multiple_of(d * BX, BX), BX)
        remote(mbuf.at[:, :, cols], mm.at[v], ms.at[0, d], mr.at[0, v], d, t).start()

    def pack_columns(s, carry):
        d = target_view(s)
        after = pl.ds(pl.multiple_of(jnp.minimum(d + 1, NV - 1) * BX, BX), BX)
        before = pl.ds(pl.multiple_of(jnp.maximum(d - 1, 0) * BX, BX), BX)
        take_after = (plane_lane < 8) & (d < NV - 1)
        take_before = (plane_lane >= 120) & (d > 0)
        for q in range(2):
            packed = jnp.zeros((TY, BX), F32)
            for k in range(8):
                z = 8 * q + k
                edge = jnp.where(
                    take_after, mbuf[z, :, after].astype(F32),
                    jnp.where(take_before, mbuf[z, :, before].astype(F32), 0.0),
                )
                packed = packed + (pltpu.roll(edge, 16 * k, 1) if k else edge)
            sq[d, q] = packed.astype(BF16)

        @pl.when(s > 0)
        def _():
            remote(sq.at[d], mq.at[v], ms.at[1, d], mr.at[1, v], d, t).start()

        return carry

    lax.fori_loop(0, NV, pack_columns, 0)
    mq[v] = sq[v]

    for s in range(1, NV):
        u = lax.rem(v + s, NV)
        remote(pb.at[u], pb.at[u], ps.at[u], pr.at[u], u, t).wait_recv()

    def small_bands(u, carry):
        z16 = pl.ds(pl.multiple_of(u * 16, 16), 16)
        for half in range(2):
            rz[half, z16, :] = toeplitz(pb[u, half : half + 1, :], 16)
            ry[half, z16, :] = toeplitz(pb[u, 2 + half : 3 + half, :], 16)
        for source, target in ((4, xf), (6, xb)):
            row = jnp.concatenate([pb[u, source : source + 1, :], pb[u, source + 1 : source + 2, :]], axis=1)
            base = toeplitz(row, 16)
            width = target.shape[-1]
            for g in range(16):
                part = (pltpu.roll(base, 16 * g, 1) if g else base)[:, :width]
                target[u, 16 * g : 16 * g + 16, :] = part.astype(BF16)
        return carry

    lax.fori_loop(0, NV, small_bands, 0)
    m = lax.broadcasted_iota(jnp.int32, (BX, 512), 0)
    n = lanes((BX, 512))
    spread_z = (m == n // 32 + 32).astype(F32)
    spread_y = (m == n % 32).astype(F32)
    for half in range(2):
        az[half] = jnp.dot(rz[half], spread_z, precision=EXACT, preferred_element_type=F32)
        ay[half] = jnp.dot(ry[half], spread_y, precision=EXACT, preferred_element_type=F32)

    def depth_rows(u, carry):
        z16 = pl.ds(pl.multiple_of(u * 16, 16), 16)
        for half, target in enumerate((wf, wb)):
            a = az[half, z16, :]
            y = ay[half, z16, :]
            for z in range(NZ):
                target[u, 16 * z : 16 * z + 16, :] = (a[z : z + 1] * y).astype(BF16)
        return carry

    lax.fori_loop(0, NV, depth_rows, 0)

    def blur(it, u):
        parts = []
        for c in range(3):
            chunk = fld[it, :, 16 * c : 16 * c + 32, :].reshape(512, 256)
            parts.append(jnp.dot(wf[u], chunk, preferred_element_type=F32).astype(BF16))
        return jnp.dot(jnp.concatenate(parts, axis=0), xf[u], preferred_element_type=F32)

    def relay_copies(u):
        return (
            (has_down, has_up, remote(su.at[u], mu.at[u], ms.at[2, u], mr.at[2, u], v, t + 1)),
            (has_up, has_down, remote(sd.at[u], md.at[u], ms.at[3, u], mr.at[3, u], v, t - 1)),
        )

    def relay(u):
        @pl.when(u != v)
        def _():
            remote(mbuf.at[:, :, pl.ds(0, BX)], mm.at[u], ms.at[0, u], mr.at[0, u], u, t).wait_recv()
            remote(sq.at[u], mq.at[u], ms.at[1, u], mr.at[1, u], u, t).wait_recv()

        for p in range(9):
            if p < 8:
                a, b = mm[u, 2 * p].astype(F32), mm[u, 2 * p + 1].astype(F32)
            else:
                a, b = mq[u, 0].astype(F32), mq[u, 1].astype(F32)
            sd[u, p] = jnp.concatenate([a[0:8], b[0:8]], axis=0).astype(BF16)
            su[u, p] = jnp.concatenate([a[24:32], b[24:32]], axis=0).astype(BF16)
        for ok_to, _, copy in relay_copies(u):
            pl.when(ok_to)(copy.start)

    ext_lane = lanes((48, BX))

    @pl.when(jnp.logical_not(has_up))
    def _():
        mu[...] = jnp.zeros(mu.shape, BF16)

    @pl.when(jnp.logical_not(has_down))
    def _():
        md[...] = jnp.zeros(md.shape, BF16)

    def ratio(values, blurred):
        return jnp.where(values > 0, values / blurred, 0.0).astype(BF16)

    def assemble(u):
        cu, cd = mu[u, 8].astype(F32), md[u, 8].astype(F32)
        for q in range(2):
            rows8 = slice(8 * q, 8 * q + 8)
            edge = jnp.concatenate([cu[rows8], mq[u, q].astype(F32), cd[rows8]], axis=0)
            for k in range(8):
                z = 8 * q + k
                side = pltpu.roll(edge, BX - 16 * k, 1) if k else edge
                side = jnp.where((ext_lane < 8) | (ext_lane >= 120), side, 0.0)
                mext[u, z, :, BX:] = side.astype(BF16)
                rt[z, :, BX:] = ratio(side, bl[u, z, :, BX:])
                r = slice(8 * (z % 2), 8 * (z % 2) + 8)
                main = jnp.concatenate(
                    [mu[u, z // 2].astype(F32)[r], mm[u, z].astype(F32), md[u, z // 2].astype(F32)[r]], axis=0
                )
                mext[u, z, :, :BX] = main.astype(BF16)
                rt[z, :, :BX] = ratio(main, bl[u, z, :, :BX])

    def correct(u, ratios):
        weight = pb[u, 8:9, :]
        rows = jnp.dot(ratios.reshape(768, 256), xb[u], preferred_element_type=F32).astype(BF16)
        rows = rows.reshape(NZ, 48, BX)
        chunks = jnp.concatenate([rows[:, 0:32].reshape(512, BX), rows[:, 16:48].reshape(512, BX)], axis=1)
        back = jnp.dot(wb[u], chunks, preferred_element_type=F32)
        for c in range(2):
            log_back = weight * jnp.log(back[:, BX * c : BX * c + BX])
            acc[:, 16 * c : 16 * c + 16, :] += log_back.reshape(NZ, 16, BX)

    count = pb[0, 8:9, :]
    for u in range(1, NV):
        count = count + pb[u, 8:9, :]

    get_own.wait()

    def relay_step(s, carry):
        relay(source_view(s))
        return carry

    lax.fori_loop(0, 4, relay_step, 0)
    receive_field(0)
    acc[...] = jnp.zeros(acc.shape, F32)

    def first_forward(s, carry):
        u = source_view(s)
        full = blur(0, u)
        for c in range(3):
            bl[u, :, 16 * c : 16 * c + 16, :] = full[256 * c : 256 * c + 256].reshape(NZ, 16, 256)
        return carry

    lax.fori_loop(0, NV, first_forward, 0)

    def first_backward(s, carry):
        u = source_view(s)
        for _, ok_from, copy in relay_copies(u):
            pl.when(ok_from)(copy.wait_recv)
        assemble(u)
        correct(u, rt[...])
        return carry

    lax.fori_loop(0, 4, first_backward, 0)
    lax.fori_loop(4, NV, relay_step, 0)
    lax.fori_loop(4, NV, first_backward, 0)
    for z in range(NZ):
        cur[z] = est[z] * jnp.exp(acc[z] / count)
    pack_field(1, cur)
    send_field(1)
    receive_field(1)
    acc[...] = jnp.zeros(acc.shape, F32)

    def second(u, carry):
        full = blur(1, u)
        for c in range(3):
            part = full[256 * c : 256 * c + 256].reshape(NZ, 16, 256)
            rt[:, 16 * c : 16 * c + 16, :] = ratio(mext[u, :, 16 * c : 16 * c + 16, :].astype(F32), part)
        correct(u, rt[...])
        return carry

    lax.fori_loop(0, NV, second, 0, unroll=8)
    for z in range(NZ):
        out[z] = cur[z] * jnp.exp(acc[z] / count)

    for it in range(ITERS):
        for ok_to, _, _, copy in field_copies(it):
            pl.when(ok_to)(copy.wait_send)

    def drain(s, carry):
        d = lax.rem(v + s, NV)

        @pl.when(d != v)
        def _():
            remote(pb.at[v], pb.at[v], ps.at[d], pr.at[d], d, t).wait_send()
            remote(mbuf.at[:, :, pl.ds(0, BX)], mm.at[v], ms.at[0, d], mr.at[0, d], d, t).wait_send()
            remote(sq.at[d], mq.at[v], ms.at[1, d], mr.at[1, d], d, t).wait_send()

        for ok_to, _, copy in relay_copies(d):
            pl.when(ok_to)(copy.wait_send)
        return carry

    lax.fori_loop(0, NV, drain, 0)


def body(estimate, measured, psf_z, psf_xy, offsets, coverage):
    scratch = [
        ((NZ, TY, NV * BX), BF16), ((NV, 16, BX), F32),
        ((2, NZ, 64, 256), BF16), ((2, 2, 64, BX), BF16), ((2, 2, 64, BX), BF16),
        ((2, 2, TY, BX), BF16), ((2, 2, TY, BX), BF16),
        ((NV, NZ, TY, BX), BF16), ((NV, 2, TY, BX), BF16), ((NV, 9, 16, BX), BF16), ((NV, 9, 16, BX), BF16),
        ((NV, 2, TY, BX), BF16), ((NV, 9, 16, BX), BF16), ((NV, 9, 16, BX), BF16),
        ((2, 128, BX), F32), ((2, 128, BX), F32), ((2, 128, 512), F32), ((2, 128, 512), F32),
        ((NV, 256, 512), BF16), ((NV, 256, 512), BF16), ((NV, 256, 256), BF16), ((NV, 256, BX), BF16),
        ((NV, NZ, 48, 256), F32), ((NV, NZ, 48, 256), BF16), ((NZ, 48, 256), BF16), ((NZ, TY, BX), F32), ((NZ, TY, BX), F32),
    ]
    dma = pltpu.SemaphoreType.DMA
    return pl.pallas_call(
        kernel,
        out_shape=jax.ShapeDtypeStruct(estimate.shape, F32),
        in_specs=[pl.BlockSpec(memory_space=pl.ANY)] * 6,
        out_specs=pl.BlockSpec(memory_space=pltpu.VMEM),
        scratch_shapes=[
            pltpu.VMEM((NZ, TY, BX), F32),
            pltpu.SMEM((1, KZ), F32),
            pltpu.SMEM((1, 2, KXY), F32),
            pltpu.SMEM((1, 2), jnp.int32),
            pltpu.SMEM((1, 1), jnp.int32),
        ]
        + [pltpu.VMEM(s, d) for s, d in scratch]
        + [dma((7,)), dma((NV,)), dma((NV,)), dma((2, 8)), dma((2, 8)), dma((4, NV)), dma((4, NV))],
        compiler_params=pltpu.CompilerParams(
            collective_id=0, has_side_effects=True, vmem_limit_bytes=60 * 1024 * 1024
        ),
    )(estimate, measured, psf_z, psf_xy, offsets, coverage)


def solution(mesh):
    placed = (
        P(None, "tile", "view"),
        P("view", None, "tile", None),
        P("view", None),
        P("view", None, None),
        P("view", None),
        P("view", "tile"),
    )
    return jax.shard_map(
        body, mesh=mesh, in_specs=placed, out_specs=P(None, "tile", "view"), check_vma=False
    )
```

```python
import functools

import jax
import jax.numpy as jnp
from jax import lax
from jax.experimental import pallas as pl
from jax.experimental.pallas import tpu as pltpu
from jax.sharding import PartitionSpec as P

MESH = pl.DeviceIdType.MESH
F32, BF16 = jnp.float32, jnp.bfloat16
SHIFT, ITERS = 4, 2
NZ, TY, BX, NV, NT = 16, 32, 128, 8, 32
KZ, KXY = 65, 9
EXACT = lax.Precision.HIGHEST


def lanes(shape):
    return lax.broadcasted_iota(jnp.int32, shape, len(shape) - 1)


def toeplitz(row, count):
    x = jnp.broadcast_to(row, (count, row.shape[-1]))
    r = lax.broadcasted_iota(jnp.int32, x.shape, 0)
    bit = 1
    while bit < count:
        x = jnp.where((r & bit) != 0, pltpu.roll(x, bit, 1), x)
        bit *= 2
    return x


def kernel(
    est_hbm, meas, pz_hbm, pxy_hbm, offs_hbm, cov_hbm, out,
    est, pz, pxy, offs, cov,
    mbuf, pb, fld, hr, hl, sr, sl, mm, mq, mu, md, sq, su, sd, sx,
    rz, ry, az, ay, wf, wb, xf, xb, bl, mext, rt, acc, cur,
    loc, ps, pr, fs, fr, ms, mr, mx,
):
    v, t = lax.axis_index("view"), lax.axis_index("tile")
    has_up, has_down = t > 0, t < NT - 1
    has_left, has_right = v > 0, v < NV - 1

    def remote(src, dst, send, recv, dv, dt):
        return pltpu.make_async_remote_copy(
            src_ref=src, dst_ref=dst, send_sem=send, recv_sem=recv, device_id=(dv, dt), device_id_type=MESH
        )

    half, spot = v // 4, lax.rem(v, 4)

    def target_view(s):
        return lax.rem(half + s // 4, 2) * 4 + lax.rem(spot + s, 4)

    def source_view(s):
        return lax.rem(half + s // 4, 2) * 4 + lax.rem(spot + 8 - s, 4)

    odd = lax.rem(t, 2) == 1
    cross = lax.rem(t + NT - 1 + 2 * lax.rem(t, 2), NT)
    straight_down = odd & (half == 1) & has_down
    straight_up = jnp.logical_not(odd) & (half == 0) & has_up

    own_cols = pl.ds(pl.multiple_of(v * BX, BX), BX)
    get_all = pltpu.make_async_copy(meas.at[0], mbuf, loc.at[0])
    get_own = pltpu.make_async_copy(meas.at[0, :, :, own_cols], mm.at[v], loc.at[1])
    small = [
        pltpu.make_async_copy(src, dst, loc.at[2 + i])
        for i, (src, dst) in enumerate(
            ((pz_hbm, pz), (pxy_hbm, pxy), (offs_hbm, offs), (cov_hbm, cov), (est_hbm, est))
        )
    ]
    for copy in small:
        copy.start()
    get_all.start()
    get_own.start()

    barrier = pltpu.get_barrier_semaphore()
    up_tile, down_tile = lax.rem(t + NT - 1, NT), lax.rem(t + 1, NT)
    partners = [(lax.rem(v + s, NV), t) for s in range(1, NV)]
    partners += [(lax.rem(v + s, NV), dt) for s in (0, 1, NV - 1) for dt in (up_tile, down_tile)]
    partners += [(lax.rem(half + 1, 2) * 4 + k, cross) for k in range(4)]
    for partner in partners:
        pl.semaphore_signal(barrier, inc=1, device_id=partner, device_id_type=MESH)
    for copy in small[:4]:
        copy.wait()

    lane1 = lanes((1, BX))
    zero1 = jnp.zeros((1, BX), F32)

    def taps(values, places):
        row = zero1
        for value, place in zip(values, places):
            row = jnp.where(lane1 == place, value, row)
        return row

    z_taps = [pz[0, i] for i in range(KZ)]
    y_taps = [pxy[0, 0, i] for i in range(KXY)]
    x_taps = [pxy[0, 1, i] for i in range(KXY)]
    oy, ox = offs[0, 0], offs[0, 1]

    def normal(values):
        return jnp.full((1, BX), functools.reduce(lambda a, b: a + b, values), F32)

    zn, yn, xn = normal(z_taps), normal(y_taps), normal(x_taps)
    rows = [
        taps(z_taps, range(KZ)) / zn,
        taps(z_taps, [KZ - 1 - i for i in range(KZ)]) / zn,
        taps(y_taps, [i + SHIFT + oy for i in range(KXY)]) / yn,
        taps(y_taps, [16 - (i + SHIFT + oy) for i in range(KXY)]) / yn,
        taps(x_taps, [4 - i - ox for i in range(KXY)]) / xn,
        taps(x_taps, [132 - i - ox for i in range(KXY)]) / xn,
        taps(x_taps, [i - 4 + ox for i in range(KXY)]) / xn,
        taps(x_taps, [i + 124 + ox for i in range(KXY)]) / xn,
        jnp.full((1, BX), cov[0, 0].astype(F32)),
    ]
    for i, row in enumerate(rows):
        pb[v, i : i + 1, :] = row
    pb[v, len(rows) :, :] = jnp.zeros((16 - len(rows), BX), F32)

    plane_lane = lanes((TY, BX))
    wide_lane = lanes((2 * TY, BX))

    def field_copies(it):
        f = fld.at[it]
        up, down, left, right = t - 1, t + 1, v - 1, v + 1
        top, low = pl.ds(0, 16), pl.ds(16, 16)
        main = pl.ds(0, BX)
        specs = [
            (has_up, has_down, f.at[:, pl.ds(16, 16), main], f.at[:, pl.ds(48, 16), main], v, up),
            (has_down, has_up, f.at[:, pl.ds(32, 16), main], f.at[:, pl.ds(0, 16), main], v, down),
        ]
        for ok_to, ok_from, s, h, dv in ((has_left, has_right, sr, hr, left), (has_right, has_left, sl, hl, right)):
            specs += [
                (ok_to, ok_from, s.at[it], h.at[it, :, pl.ds(16, 32)], dv, t),
                (ok_to & has_up, ok_from & has_down, s.at[it, :, top], h.at[it, :, pl.ds(48, 16)], dv, up),
                (ok_to & has_down, ok_from & has_up, s.at[it, :, low], h.at[it, :, pl.ds(0, 16)], dv, down),
            ]
        return [
            (ok_to, ok_from, dst, remote(src, dst, fs.at[it, i], fr.at[it, i], dv, dt))
            for i, (ok_to, ok_from, src, dst, dv, dt) in enumerate(specs)
        ]

    def pack_field(it, source):
        for z in range(NZ):
            fld[it, z, 16:48, 0:BX] = source[z].astype(BF16)

    def pack_sides(it, source):
        for q in range(2):
            head = jnp.zeros((TY, BX), F32)
            tail = jnp.zeros((TY, BX), F32)
            for k in range(8):
                rolled = source[8 * q + k]
                if k:
                    rolled = pltpu.roll(rolled, 16 * k, 1)
                head = jnp.where(plane_lane // 16 == k, rolled, head)
                tail = jnp.where(plane_lane // 16 == (k + 7) % 8, rolled, tail)
            sr[it, q] = head.astype(BF16)
            sl[it, q] = tail.astype(BF16)

    def send_field(it, which):
        for ok_to, _, _, copy in field_copies(it)[which]:
            pl.when(ok_to)(copy.start)

    rows, sides = slice(0, 2), slice(2, 8)

    def arrived(it, which):
        for _, ok_from, dst, copy in field_copies(it)[which]:
            pl.when(ok_from)(copy.wait_recv)

            @pl.when(jnp.logical_not(ok_from))
            def _():
                dst[...] = jnp.zeros(dst.shape, BF16)

    def receive_field(it):
        arrived(it, sides)
        for q in range(2):
            right = hr[it, q].astype(F32)
            left = hl[it, q].astype(F32)
            for k in range(8):
                both = jnp.where(wide_lane // 16 == k, right, left)
                if k:
                    both = pltpu.roll(both, BX - 16 * k, 1)
                both = jnp.where((wide_lane < 16) | (wide_lane >= 112), both, 0.0)
                fld[it, 8 * q + k, :, BX:] = both.astype(BF16)
        arrived(it, rows)

    small[4].wait()
    pack_field(0, est)
    pack_sides(0, est)
    get_all.wait()

    pl.semaphore_wait(barrier, len(partners))
    for s in range(1, NV):
        d = target_view(s)
        remote(pb.at[v], pb.at[v], ps.at[d], pr.at[v], d, t).start()
    send_field(0, slice(0, 8))
    for s in range(1, NV):
        d = target_view(s)
        cols = pl.ds(pl.multiple_of(d * BX, BX), BX)
        remote(mbuf.at[:, :, cols], mm.at[v], ms.at[0, d], mr.at[0, v], d, t).start()

    def straight_copies(d):
        return (
            (straight_down, remote(sx.at[d], mu.at[v], mx.at[d], mr.at[2, v], d, t + 1)),
            (straight_up, remote(sx.at[d], md.at[v], mx.at[d], mr.at[3, v], d, t - 1)),
        )

    def pack_columns(s, carry):
        d = target_view(s)
        after = pl.ds(pl.multiple_of(jnp.minimum(d + 1, NV - 1) * BX, BX), BX)
        before = pl.ds(pl.multiple_of(jnp.maximum(d - 1, 0) * BX, BX), BX)
        take_after = (plane_lane < 8) & (d < NV - 1)
        take_before = (plane_lane >= 120) & (d > 0)
        corner = []
        for q in range(2):
            packed = jnp.zeros((TY, BX), F32)
            for k in range(8):
                z = 8 * q + k
                edge = jnp.where(
                    take_after, mbuf[z, :, after].astype(F32),
                    jnp.where(take_before, mbuf[z, :, before].astype(F32), 0.0),
                )
                packed = packed + (pltpu.roll(edge, 16 * k, 1) if k else edge)
            corner.append(packed)
            sq[d, q] = packed.astype(BF16)

        @pl.when(s > 0)
        def _():
            remote(sq.at[d], mq.at[v], ms.at[1, d], mr.at[1, v], d, t).start()

        @pl.when((s >= 4) & (straight_up | straight_down))
        def _():
            here = pl.ds(pl.multiple_of(d * BX, BX), BX)

            def edge_rows(a):
                return jnp.where(odd, a[24:32], a[0:8])

            for p in range(9):
                if p < 8:
                    a, b = mbuf[2 * p, :, here].astype(F32), mbuf[2 * p + 1, :, here].astype(F32)
                else:
                    a, b = corner
                sx[d, p] = jnp.concatenate([edge_rows(a), edge_rows(b)], axis=0).astype(BF16)
            for ok_to, copy in straight_copies(d):
                pl.when(ok_to)(copy.start)

        return carry

    lax.fori_loop(0, NV, pack_columns, 0)
    mq[v] = sq[v]

    for s in range(1, NV):
        u = lax.rem(v + s, NV)
        remote(pb.at[u], pb.at[u], ps.at[u], pr.at[u], u, t).wait_recv()

    def small_bands(u, carry):
        z16 = pl.ds(pl.multiple_of(u * 16, 16), 16)
        for half in range(2):
            rz[half, z16, :] = toeplitz(pb[u, half : half + 1, :], 16)
            ry[half, z16, :] = toeplitz(pb[u, 2 + half : 3 + half, :], 16)
        for source, target in ((4, xf), (6, xb)):
            row = jnp.concatenate([pb[u, source : source + 1, :], pb[u, source + 1 : source + 2, :]], axis=1)
            base = toeplitz(row, 16)
            width = target.shape[-1]
            for g in range(16):
                part = (pltpu.roll(base, 16 * g, 1) if g else base)[:, :width]
                target[u, 16 * g : 16 * g + 16, :] = part.astype(BF16)
        return carry

    lax.fori_loop(0, NV, small_bands, 0)
    m = lax.broadcasted_iota(jnp.int32, (BX, 512), 0)
    n = lanes((BX, 512))
    spread_z = (m == n // 32 + 32).astype(F32)
    spread_y = (m == n % 32).astype(F32)
    for way in range(2):
        az[way] = jnp.dot(rz[way], spread_z, precision=EXACT, preferred_element_type=F32)
        ay[way] = jnp.dot(ry[way], spread_y, precision=EXACT, preferred_element_type=F32)

    def depth_rows(u, carry):
        z16 = pl.ds(pl.multiple_of(u * 16, 16), 16)
        for half, target in enumerate((wf, wb)):
            a = az[half, z16, :]
            y = ay[half, z16, :]
            for z in range(NZ):
                target[u, 16 * z : 16 * z + 16, :] = (a[z : z + 1] * y).astype(BF16)
        return carry

    lax.fori_loop(0, NV, depth_rows, 0)

    def blur(it, u):
        parts = []
        for c in range(3):
            chunk = fld[it, :, 16 * c : 16 * c + 32, :].reshape(512, 256)
            parts.append(jnp.dot(wf[u], chunk, preferred_element_type=F32).astype(BF16))
        return jnp.dot(jnp.concatenate(parts, axis=0), xf[u], preferred_element_type=F32)

    def relay_copies(u):
        far = u // 4 != half
        skip_down = far & odd & (half == 0)
        skip_up = far & jnp.logical_not(odd) & (half == 1)
        return (
            (has_down & jnp.logical_not(skip_down), has_up, remote(su.at[u], mu.at[u], ms.at[2, u], mr.at[2, u], v, t + 1)),
            (has_up & jnp.logical_not(skip_up), has_down, remote(sd.at[u], md.at[u], ms.at[3, u], mr.at[3, u], v, t - 1)),
        )

    def relay(u):
        @pl.when(u != v)
        def _():
            remote(mbuf.at[:, :, pl.ds(0, BX)], mm.at[u], ms.at[0, u], mr.at[0, u], u, t).wait_recv()
            remote(sq.at[u], mq.at[u], ms.at[1, u], mr.at[1, u], u, t).wait_recv()

        for p in range(9):
            if p < 8:
                a, b = mm[u, 2 * p].astype(F32), mm[u, 2 * p + 1].astype(F32)
            else:
                a, b = mq[u, 0].astype(F32), mq[u, 1].astype(F32)
            sd[u, p] = jnp.concatenate([a[0:8], b[0:8]], axis=0).astype(BF16)
            su[u, p] = jnp.concatenate([a[24:32], b[24:32]], axis=0).astype(BF16)
        for ok_to, _, copy in relay_copies(u):
            pl.when(ok_to)(copy.start)

    ext_lane = lanes((48, BX))

    @pl.when(jnp.logical_not(has_up))
    def _():
        mu[...] = jnp.zeros(mu.shape, BF16)

    @pl.when(jnp.logical_not(has_down))
    def _():
        md[...] = jnp.zeros(md.shape, BF16)

    def ratio(values, blurred):
        return jnp.where(values > 0, values / blurred, 0.0).astype(BF16)

    def assemble(u):
        cu, cd = mu[u, 8].astype(F32), md[u, 8].astype(F32)
        for q in range(2):
            rows8 = slice(8 * q, 8 * q + 8)
            edge = jnp.concatenate([cu[rows8], mq[u, q].astype(F32), cd[rows8]], axis=0)
            for k in range(8):
                z = 8 * q + k
                side = pltpu.roll(edge, BX - 16 * k, 1) if k else edge
                side = jnp.where((ext_lane < 8) | (ext_lane >= 120), side, 0.0)
                mext[u, z, :, BX:] = side.astype(BF16)
                rt[z, :, BX:] = ratio(side, bl[u, z, :, BX:])
                r = slice(8 * (z % 2), 8 * (z % 2) + 8)
                main = jnp.concatenate(
                    [mu[u, z // 2].astype(F32)[r], mm[u, z].astype(F32), md[u, z // 2].astype(F32)[r]], axis=0
                )
                mext[u, z, :, :BX] = main.astype(BF16)
                rt[z, :, :BX] = ratio(main, bl[u, z, :, :BX])

    def correct(u, ratios):
        weight = pb[u, 8:9, :]
        rows = jnp.dot(ratios.reshape(768, 256), xb[u], preferred_element_type=F32).astype(BF16)
        rows = rows.reshape(NZ, 48, BX)
        chunks = jnp.concatenate([rows[:, 0:32].reshape(512, BX), rows[:, 16:48].reshape(512, BX)], axis=1)
        back = jnp.dot(wb[u], chunks, preferred_element_type=F32)
        for c in range(2):
            log_back = weight * jnp.log(back[:, BX * c : BX * c + BX])
            acc[:, 16 * c : 16 * c + 16, :] += log_back.reshape(NZ, 16, BX)

    count = pb[0, 8:9, :]
    for u in range(1, NV):
        count = count + pb[u, 8:9, :]

    get_own.wait()

    def relay_step(s, carry):
        relay(source_view(s))
        return carry

    lax.fori_loop(0, 4, relay_step, 0)
    receive_field(0)
    acc[...] = jnp.zeros(acc.shape, F32)

    def first_forward(s, carry):
        u = source_view(s)
        full = blur(0, u)
        for c in range(3):
            bl[u, :, 16 * c : 16 * c + 16, :] = full[256 * c : 256 * c + 256].reshape(NZ, 16, 256)
        return carry

    lax.fori_loop(0, NV, first_forward, 0)

    def first_backward(s, carry):
        u = source_view(s)
        for _, ok_from, copy in relay_copies(u):
            pl.when(ok_from)(copy.wait_recv)
        assemble(u)
        correct(u, rt[...])
        return carry

    lax.fori_loop(0, 4, first_backward, 0)
    lax.fori_loop(4, NV, relay_step, 0)
    lax.fori_loop(4, NV, first_backward, 0)
    for z in range(NZ):
        cur[z] = est[z] * jnp.exp(acc[z] / count)
    pack_field(1, cur)
    send_field(1, rows)
    pack_sides(1, cur)
    send_field(1, sides)
    acc[...] = jnp.zeros(acc.shape, F32)

    def drain(s, carry):
        d = lax.rem(v + s, NV)

        @pl.when(d != v)
        def _():
            remote(pb.at[v], pb.at[v], ps.at[d], pr.at[d], d, t).wait_send()
            remote(mbuf.at[:, :, pl.ds(0, BX)], mm.at[v], ms.at[0, d], mr.at[0, d], d, t).wait_send()
            remote(sq.at[d], mq.at[v], ms.at[1, d], mr.at[1, d], d, t).wait_send()

        for ok_to, _, copy in relay_copies(d):
            pl.when(ok_to)(copy.wait_send)
        for ok_to, copy in straight_copies(d):
            pl.when(ok_to & (d // 4 != half))(copy.wait_send)
        return carry

    lax.fori_loop(0, NV, drain, 0)

    receive_field(1)

    def second(u, carry):
        full = blur(1, u)
        for c in range(3):
            part = full[256 * c : 256 * c + 256].reshape(NZ, 16, 256)
            rt[:, 16 * c : 16 * c + 16, :] = ratio(mext[u, :, 16 * c : 16 * c + 16, :].astype(F32), part)
        correct(u, rt[...])
        return carry

    lax.fori_loop(0, NV, second, 0, unroll=8)
    for z in range(NZ):
        out[z] = cur[z] * jnp.exp(acc[z] / count)

    for it in range(ITERS):
        for ok_to, _, _, copy in field_copies(it):
            pl.when(ok_to)(copy.wait_send)


def body(estimate, measured, psf_z, psf_xy, offsets, coverage):
    scratch = [
        ((NZ, TY, NV * BX), BF16), ((NV, 16, BX), F32),
        ((2, NZ, 64, 256), BF16), ((2, 2, 64, BX), BF16), ((2, 2, 64, BX), BF16),
        ((2, 2, TY, BX), BF16), ((2, 2, TY, BX), BF16),
        ((NV, NZ, TY, BX), BF16), ((NV, 2, TY, BX), BF16), ((NV, 9, 16, BX), BF16), ((NV, 9, 16, BX), BF16),
        ((NV, 2, TY, BX), BF16), ((NV, 9, 16, BX), BF16), ((NV, 9, 16, BX), BF16), ((NV, 9, 16, BX), BF16),
        ((2, 128, BX), F32), ((2, 128, BX), F32), ((2, 128, 512), F32), ((2, 128, 512), F32),
        ((NV, 256, 512), BF16), ((NV, 256, 512), BF16), ((NV, 256, 256), BF16), ((NV, 256, BX), BF16),
        ((NV, NZ, 48, 256), F32), ((NV, NZ, 48, 256), BF16), ((NZ, 48, 256), BF16), ((NZ, TY, BX), F32), ((NZ, TY, BX), F32),
    ]
    dma = pltpu.SemaphoreType.DMA
    return pl.pallas_call(
        kernel,
        out_shape=jax.ShapeDtypeStruct(estimate.shape, F32),
        in_specs=[pl.BlockSpec(memory_space=pl.ANY)] * 6,
        out_specs=pl.BlockSpec(memory_space=pltpu.VMEM),
        scratch_shapes=[
            pltpu.VMEM((NZ, TY, BX), F32),
            pltpu.SMEM((1, KZ), F32),
            pltpu.SMEM((1, 2, KXY), F32),
            pltpu.SMEM((1, 2), jnp.int32),
            pltpu.SMEM((1, 1), jnp.int32),
        ]
        + [pltpu.VMEM(s, d) for s, d in scratch]
        + [dma((7,)), dma((NV,)), dma((NV,)), dma((2, 8)), dma((2, 8)), dma((4, NV)), dma((4, NV)), dma((NV,))],
        compiler_params=pltpu.CompilerParams(
            collective_id=0, has_side_effects=True, vmem_limit_bytes=60 * 1024 * 1024
        ),
    )(estimate, measured, psf_z, psf_xy, offsets, coverage)


def solution(mesh):
    placed = (
        P(None, "tile", "view"),
        P("view", None, "tile", None),
        P("view", None),
        P("view", None, None),
        P("view", None),
        P("view", "tile"),
    )
    return jax.shard_map(
        body, mesh=mesh, in_specs=placed, out_specs=P(None, "tile", "view"), check_vma=False
    )
```

```python
import functools

import jax
import jax.numpy as jnp
from jax import lax
from jax.experimental import pallas as pl
from jax.experimental.pallas import tpu as pltpu
from jax.sharding import PartitionSpec as P

MESH = pl.DeviceIdType.MESH
F32, BF16 = jnp.float32, jnp.bfloat16
SHIFT, ITERS = 4, 2
NZ, TY, BX, NV, NT = 16, 32, 128, 8, 32
KZ, KXY = 65, 9
EXACT = lax.Precision.HIGHEST


def lanes(shape):
    return lax.broadcasted_iota(jnp.int32, shape, len(shape) - 1)


def toeplitz(row, count):
    x = jnp.broadcast_to(row, (count, row.shape[-1]))
    r = lax.broadcasted_iota(jnp.int32, x.shape, 0)
    bit = 1
    while bit < count:
        x = jnp.where((r & bit) != 0, pltpu.roll(x, bit, 1), x)
        bit *= 2
    return x


def kernel(
    est_hbm, meas, pz_hbm, pxy_hbm, offs_hbm, cov_hbm, out,
    est, pz, pxy, offs, cov,
    mbuf, pb, fld, hr, hl, sr, sl, mm, mq, mu, md, sq, su, sd, sx,
    rz, ry, az, ay, wf, wb, xf, xb, bl, mext, rt, acc, cur,
    loc, ps, pr, fs, fr, ms, mr, mx,
):
    v, t = lax.axis_index("view"), lax.axis_index("tile")
    has_up, has_down = t > 0, t < NT - 1
    has_left, has_right = v > 0, v < NV - 1

    def remote(src, dst, send, recv, dv, dt):
        return pltpu.make_async_remote_copy(
            src_ref=src, dst_ref=dst, send_sem=send, recv_sem=recv, device_id=(dv, dt), device_id_type=MESH
        )

    half, spot = v // 4, lax.rem(v, 4)

    def target_view(s):
        return lax.rem(half + s // 4, 2) * 4 + lax.rem(spot + s, 4)

    def source_view(s):
        return lax.rem(half + s // 4, 2) * 4 + lax.rem(spot + 8 - s, 4)

    odd = lax.rem(t, 2) == 1
    cross = lax.rem(t + NT - 1 + 2 * lax.rem(t, 2), NT)
    straight_down = odd & (half == 1) & has_down
    straight_up = jnp.logical_not(odd) & (half == 0) & has_up

    own_cols = pl.ds(pl.multiple_of(v * BX, BX), BX)
    get_all = pltpu.make_async_copy(meas.at[0], mbuf, loc.at[0])
    get_own = pltpu.make_async_copy(meas.at[0, :, :, own_cols], mm.at[v], loc.at[1])
    small = [
        pltpu.make_async_copy(src, dst, loc.at[2 + i])
        for i, (src, dst) in enumerate(
            ((pz_hbm, pz), (pxy_hbm, pxy), (offs_hbm, offs), (cov_hbm, cov), (est_hbm, est))
        )
    ]
    for copy in small:
        copy.start()
    get_all.start()
    get_own.start()

    barrier = pltpu.get_barrier_semaphore()
    up_tile, down_tile = lax.rem(t + NT - 1, NT), lax.rem(t + 1, NT)
    partners = [(lax.rem(v + s, NV), t) for s in range(1, NV)]
    partners += [(lax.rem(v + s, NV), dt) for s in (0, 1, NV - 1) for dt in (up_tile, down_tile)]
    partners += [(lax.rem(half + 1, 2) * 4 + k, cross) for k in range(4)]
    for partner in partners:
        pl.semaphore_signal(barrier, inc=1, device_id=partner, device_id_type=MESH)
    for copy in small[:4]:
        copy.wait()

    lane1 = lanes((1, BX))
    zero1 = jnp.zeros((1, BX), F32)

    def taps(values, places):
        row = zero1
        for value, place in zip(values, places):
            row = jnp.where(lane1 == place, value, row)
        return row

    z_taps = [pz[0, i] for i in range(KZ)]
    y_taps = [pxy[0, 0, i] for i in range(KXY)]
    x_taps = [pxy[0, 1, i] for i in range(KXY)]
    oy, ox = offs[0, 0], offs[0, 1]

    def normal(values):
        return jnp.full((1, BX), functools.reduce(lambda a, b: a + b, values), F32)

    zn, yn, xn = normal(z_taps), normal(y_taps), normal(x_taps)
    rows = [
        taps(z_taps, range(KZ)) / zn,
        taps(z_taps, [KZ - 1 - i for i in range(KZ)]) / zn,
        taps(y_taps, [i + SHIFT + oy for i in range(KXY)]) / yn,
        taps(y_taps, [16 - (i + SHIFT + oy) for i in range(KXY)]) / yn,
        taps(x_taps, [4 - i - ox for i in range(KXY)]) / xn,
        taps(x_taps, [132 - i - ox for i in range(KXY)]) / xn,
        taps(x_taps, [i - 4 + ox for i in range(KXY)]) / xn,
        taps(x_taps, [i + 124 + ox for i in range(KXY)]) / xn,
        jnp.full((1, BX), cov[0, 0].astype(F32)),
    ]
    for i, row in enumerate(rows):
        pb[v, i : i + 1, :] = row
    pb[v, len(rows) :, :] = jnp.zeros((16 - len(rows), BX), F32)

    plane_lane = lanes((TY, BX))
    wide_lane = lanes((2 * TY, BX))

    def field_copies(it):
        f = fld.at[it]
        up, down, left, right = t - 1, t + 1, v - 1, v + 1
        top, low = pl.ds(0, 16), pl.ds(16, 16)
        main = pl.ds(0, BX)
        specs = [
            (has_up, has_down, f.at[:, pl.ds(16, 16), main], f.at[:, pl.ds(48, 16), main], v, up),
            (has_down, has_up, f.at[:, pl.ds(32, 16), main], f.at[:, pl.ds(0, 16), main], v, down),
        ]
        for ok_to, ok_from, s, h, dv in ((has_left, has_right, sr, hr, left), (has_right, has_left, sl, hl, right)):
            specs += [
                (ok_to, ok_from, s.at[it], h.at[it, :, pl.ds(16, 32)], dv, t),
                (ok_to & has_up, ok_from & has_down, s.at[it, :, top], h.at[it, :, pl.ds(48, 16)], dv, up),
                (ok_to & has_down, ok_from & has_up, s.at[it, :, low], h.at[it, :, pl.ds(0, 16)], dv, down),
            ]
        return [
            (ok_to, ok_from, dst, remote(src, dst, fs.at[it, i], fr.at[it, i], dv, dt))
            for i, (ok_to, ok_from, src, dst, dv, dt) in enumerate(specs)
        ]

    def pack_field(it, source):
        for z in range(NZ):
            fld[it, z, 16:48, 0:BX] = source[z].astype(BF16)

    def pack_sides(it, source):
        for q in range(2):
            head = jnp.zeros((TY, BX), F32)
            tail = jnp.zeros((TY, BX), F32)
            for k in range(8):
                rolled = source[8 * q + k]
                if k:
                    rolled = pltpu.roll(rolled, 16 * k, 1)
                head = jnp.where(plane_lane // 16 == k, rolled, head)
                tail = jnp.where(plane_lane // 16 == (k + 7) % 8, rolled, tail)
            sr[it, q] = head.astype(BF16)
            sl[it, q] = tail.astype(BF16)

    def send_field(it, which):
        for ok_to, _, _, copy in field_copies(it)[which]:
            pl.when(ok_to)(copy.start)

    rows, sides = slice(0, 2), slice(2, 8)

    def arrived(it, which):
        for _, ok_from, dst, copy in field_copies(it)[which]:
            pl.when(ok_from)(copy.wait_recv)

            @pl.when(jnp.logical_not(ok_from))
            def _():
                dst[...] = jnp.zeros(dst.shape, BF16)

    def receive_field(it):
        arrived(it, sides)
        for q in range(2):
            right = hr[it, q].astype(F32)
            left = hl[it, q].astype(F32)
            for k in range(8):
                both = jnp.where(wide_lane // 16 == k, right, left)
                if k:
                    both = pltpu.roll(both, BX - 16 * k, 1)
                both = jnp.where((wide_lane < 16) | (wide_lane >= 112), both, 0.0)
                fld[it, 8 * q + k, :, BX:] = both.astype(BF16)
        arrived(it, rows)

    small[4].wait()
    pack_field(0, est)
    pack_sides(0, est)
    get_all.wait()

    pl.semaphore_wait(barrier, len(partners))
    for s in range(1, NV):
        d = target_view(s)
        remote(pb.at[v], pb.at[v], ps.at[d], pr.at[v], d, t).start()
    send_field(0, slice(0, 8))
    for s in range(1, NV):
        d = target_view(s)
        cols = pl.ds(pl.multiple_of(d * BX, BX), BX)
        remote(mbuf.at[:, :, cols], mm.at[v], ms.at[0, d], mr.at[0, v], d, t).start()

    def straight_copies(d):
        return (
            (straight_down, remote(sx.at[d], mu.at[v], mx.at[d], mr.at[2, v], d, t + 1)),
            (straight_up, remote(sx.at[d], md.at[v], mx.at[d], mr.at[3, v], d, t - 1)),
        )

    def pack_columns(s, carry):
        d = target_view(s)
        after = pl.ds(pl.multiple_of(jnp.minimum(d + 1, NV - 1) * BX, BX), BX)
        before = pl.ds(pl.multiple_of(jnp.maximum(d - 1, 0) * BX, BX), BX)
        take_after = (plane_lane < 8) & (d < NV - 1)
        take_before = (plane_lane >= 120) & (d > 0)
        corner = []
        for q in range(2):
            packed = jnp.zeros((TY, BX), F32)
            for k in range(8):
                z = 8 * q + k
                edge = jnp.where(
                    take_after, mbuf[z, :, after].astype(F32),
                    jnp.where(take_before, mbuf[z, :, before].astype(F32), 0.0),
                )
                packed = packed + (pltpu.roll(edge, 16 * k, 1) if k else edge)
            corner.append(packed)
            sq[d, q] = packed.astype(BF16)

        @pl.when(s > 0)
        def _():
            remote(sq.at[d], mq.at[v], ms.at[1, d], mr.at[1, v], d, t).start()

        @pl.when((s >= 4) & (straight_up | straight_down))
        def _():
            here = pl.ds(pl.multiple_of(d * BX, BX), BX)

            def edge_rows(a):
                return jnp.where(odd, a[24:32], a[0:8])

            for p in range(9):
                if p < 8:
                    a, b = mbuf[2 * p, :, here].astype(F32), mbuf[2 * p + 1, :, here].astype(F32)
                else:
                    a, b = corner
                sx[d, p] = jnp.concatenate([edge_rows(a), edge_rows(b)], axis=0).astype(BF16)
            for ok_to, copy in straight_copies(d):
                pl.when(ok_to)(copy.start)

        return carry

    lax.fori_loop(0, NV, pack_columns, 0)
    mq[v] = sq[v]

    for s in range(1, NV):
        u = lax.rem(v + s, NV)
        remote(pb.at[u], pb.at[u], ps.at[u], pr.at[u], u, t).wait_recv()

    def small_bands(u, carry):
        z16 = pl.ds(pl.multiple_of(u * 16, 16), 16)
        for half in range(2):
            rz[half, z16, :] = toeplitz(pb[u, half : half + 1, :], 16)
            ry[half, z16, :] = toeplitz(pb[u, 2 + half : 3 + half, :], 16)
        for source, target in ((4, xf), (6, xb)):
            row = jnp.concatenate([pb[u, source : source + 1, :], pb[u, source + 1 : source + 2, :]], axis=1)
            base = toeplitz(row, 16)
            width = target.shape[-1]
            for g in range(16):
                part = (pltpu.roll(base, 16 * g, 1) if g else base)[:, :width]
                target[u, 16 * g : 16 * g + 16, :] = part.astype(BF16)
        return carry

    lax.fori_loop(0, NV, small_bands, 0)
    m = lax.broadcasted_iota(jnp.int32, (BX, 512), 0)
    n = lanes((BX, 512))
    spread_z = (m == n // 32 + 32).astype(F32)
    spread_y = (m == n % 32).astype(F32)
    for way in range(2):
        az[way] = jnp.dot(rz[way], spread_z, precision=EXACT, preferred_element_type=F32)
        ay[way] = jnp.dot(ry[way], spread_y, precision=EXACT, preferred_element_type=F32)

    def depth_rows(u, carry):
        z16 = pl.ds(pl.multiple_of(u * 16, 16), 16)
        for half, target in enumerate((wf, wb)):
            a = az[half, z16, :]
            y = ay[half, z16, :]
            for z in range(NZ):
                target[u, 16 * z : 16 * z + 16, :] = (a[z : z + 1] * y).astype(BF16)
        return carry

    lax.fori_loop(0, NV, depth_rows, 0)

    def blur(it, u):
        parts = []
        for c in range(3):
            chunk = fld[it, :, 16 * c : 16 * c + 32, :].reshape(512, 256)
            parts.append(jnp.dot(wf[u], chunk, preferred_element_type=F32).astype(BF16))
        return jnp.dot(jnp.concatenate(parts, axis=0), xf[u], preferred_element_type=F32)

    def relay_copies(u):
        far = u // 4 != half
        skip_down = far & odd & (half == 0)
        skip_up = far & jnp.logical_not(odd) & (half == 1)
        return (
            (has_down & jnp.logical_not(skip_down), has_up, remote(su.at[u], mu.at[u], ms.at[2, u], mr.at[2, u], v, t + 1)),
            (has_up & jnp.logical_not(skip_up), has_down, remote(sd.at[u], md.at[u], ms.at[3, u], mr.at[3, u], v, t - 1)),
        )

    def relay(u):
        @pl.when(u != v)
        def _():
            remote(mbuf.at[:, :, pl.ds(0, BX)], mm.at[u], ms.at[0, u], mr.at[0, u], u, t).wait_recv()
            remote(sq.at[u], mq.at[u], ms.at[1, u], mr.at[1, u], u, t).wait_recv()

        for p in range(9):
            if p < 8:
                a, b = mm[u, 2 * p].astype(F32), mm[u, 2 * p + 1].astype(F32)
            else:
                a, b = mq[u, 0].astype(F32), mq[u, 1].astype(F32)
            sd[u, p] = jnp.concatenate([a[0:8], b[0:8]], axis=0).astype(BF16)
            su[u, p] = jnp.concatenate([a[24:32], b[24:32]], axis=0).astype(BF16)
        for ok_to, _, copy in relay_copies(u):
            pl.when(ok_to)(copy.start)

    ext_lane = lanes((48, BX))

    @pl.when(jnp.logical_not(has_up))
    def _():
        mu[...] = jnp.zeros(mu.shape, BF16)

    @pl.when(jnp.logical_not(has_down))
    def _():
        md[...] = jnp.zeros(md.shape, BF16)

    def ratio(values, blurred):
        return jnp.where(values > 0, values / blurred, 0.0).astype(BF16)

    def assemble(u):
        cu, cd = mu[u, 8].astype(F32), md[u, 8].astype(F32)
        for q in range(2):
            rows8 = slice(8 * q, 8 * q + 8)
            edge = jnp.concatenate([cu[rows8], mq[u, q].astype(F32), cd[rows8]], axis=0)
            for k in range(8):
                z = 8 * q + k
                side = pltpu.roll(edge, BX - 16 * k, 1) if k else edge
                side = jnp.where((ext_lane < 8) | (ext_lane >= 120), side, 0.0)
                mext[u, z, :, BX:] = side.astype(BF16)
                rt[z, :, BX:] = ratio(side, bl[u, z, :, BX:])
                r = slice(8 * (z % 2), 8 * (z % 2) + 8)
                main = jnp.concatenate(
                    [mu[u, z // 2].astype(F32)[r], mm[u, z].astype(F32), md[u, z // 2].astype(F32)[r]], axis=0
                )
                mext[u, z, :, :BX] = main.astype(BF16)
                rt[z, :, :BX] = ratio(main, bl[u, z, :, :BX])

    def correct(u, ratios):
        weight = pb[u, 8:9, :]
        rows = jnp.dot(ratios.reshape(768, 256), xb[u], preferred_element_type=F32).astype(BF16)
        rows = rows.reshape(NZ, 48, BX)
        chunks = jnp.concatenate([rows[:, 0:32].reshape(512, BX), rows[:, 16:48].reshape(512, BX)], axis=1)
        back = jnp.dot(wb[u], chunks, preferred_element_type=F32)
        for c in range(2):
            log_back = weight * jnp.log(back[:, BX * c : BX * c + BX])
            acc[:, 16 * c : 16 * c + 16, :] += log_back.reshape(NZ, 16, BX)

    count = pb[0, 8:9, :]
    for u in range(1, NV):
        count = count + pb[u, 8:9, :]

    get_own.wait()

    def relay_step(s, carry):
        relay(source_view(s))
        return carry

    lax.fori_loop(0, 4, relay_step, 0)
    receive_field(0)
    acc[...] = jnp.zeros(acc.shape, F32)

    def first_forward(s, carry):
        u = source_view(s)
        full = blur(0, u)
        for c in range(3):
            bl[u, :, 16 * c : 16 * c + 16, :] = full[256 * c : 256 * c + 256].reshape(NZ, 16, 256)
        return carry

    lax.fori_loop(0, NV, first_forward, 0, unroll=8)

    def first_backward(s, carry):
        u = source_view(s)
        for _, ok_from, copy in relay_copies(u):
            pl.when(ok_from)(copy.wait_recv)
        assemble(u)
        correct(u, rt[...])
        return carry

    lax.fori_loop(4, NV, relay_step, 0)
    lax.fori_loop(0, NV, first_backward, 0, unroll=4)
    for z in range(NZ):
        cur[z] = est[z] * jnp.exp(acc[z] / count)
    pack_field(1, cur)
    send_field(1, rows)
    pack_sides(1, cur)
    send_field(1, sides)
    acc[...] = jnp.zeros(acc.shape, F32)

    def drain(s, carry):
        d = lax.rem(v + s, NV)

        @pl.when(d != v)
        def _():
            remote(pb.at[v], pb.at[v], ps.at[d], pr.at[d], d, t).wait_send()
            remote(mbuf.at[:, :, pl.ds(0, BX)], mm.at[v], ms.at[0, d], mr.at[0, d], d, t).wait_send()
            remote(sq.at[d], mq.at[v], ms.at[1, d], mr.at[1, d], d, t).wait_send()

        for ok_to, _, copy in relay_copies(d):
            pl.when(ok_to)(copy.wait_send)
        for ok_to, copy in straight_copies(d):
            pl.when(ok_to & (d // 4 != half))(copy.wait_send)
        return carry

    lax.fori_loop(0, NV, drain, 0)

    receive_field(1)

    def second(u, carry):
        full = blur(1, u)
        for c in range(3):
            part = full[256 * c : 256 * c + 256].reshape(NZ, 16, 256)
            rt[:, 16 * c : 16 * c + 16, :] = ratio(mext[u, :, 16 * c : 16 * c + 16, :].astype(F32), part)
        correct(u, rt[...])
        return carry

    lax.fori_loop(0, NV, second, 0, unroll=8)
    for z in range(NZ):
        out[z] = cur[z] * jnp.exp(acc[z] / count)

    for it in range(ITERS):
        for ok_to, _, _, copy in field_copies(it):
            pl.when(ok_to)(copy.wait_send)


def body(estimate, measured, psf_z, psf_xy, offsets, coverage):
    scratch = [
        ((NZ, TY, NV * BX), BF16), ((NV, 16, BX), F32),
        ((2, NZ, 64, 256), BF16), ((2, 2, 64, BX), BF16), ((2, 2, 64, BX), BF16),
        ((2, 2, TY, BX), BF16), ((2, 2, TY, BX), BF16),
        ((NV, NZ, TY, BX), BF16), ((NV, 2, TY, BX), BF16), ((NV, 9, 16, BX), BF16), ((NV, 9, 16, BX), BF16),
        ((NV, 2, TY, BX), BF16), ((NV, 9, 16, BX), BF16), ((NV, 9, 16, BX), BF16), ((NV, 9, 16, BX), BF16),
        ((2, 128, BX), F32), ((2, 128, BX), F32), ((2, 128, 512), F32), ((2, 128, 512), F32),
        ((NV, 256, 512), BF16), ((NV, 256, 512), BF16), ((NV, 256, 256), BF16), ((NV, 256, BX), BF16),
        ((NV, NZ, 48, 256), F32), ((NV, NZ, 48, 256), BF16), ((NZ, 48, 256), BF16), ((NZ, TY, BX), F32), ((NZ, TY, BX), F32),
    ]
    dma = pltpu.SemaphoreType.DMA
    return pl.pallas_call(
        kernel,
        out_shape=jax.ShapeDtypeStruct(estimate.shape, F32),
        in_specs=[pl.BlockSpec(memory_space=pl.ANY)] * 6,
        out_specs=pl.BlockSpec(memory_space=pltpu.VMEM),
        scratch_shapes=[
            pltpu.VMEM((NZ, TY, BX), F32),
            pltpu.SMEM((1, KZ), F32),
            pltpu.SMEM((1, 2, KXY), F32),
            pltpu.SMEM((1, 2), jnp.int32),
            pltpu.SMEM((1, 1), jnp.int32),
        ]
        + [pltpu.VMEM(s, d) for s, d in scratch]
        + [dma((7,)), dma((NV,)), dma((NV,)), dma((2, 8)), dma((2, 8)), dma((4, NV)), dma((4, NV)), dma((NV,))],
        compiler_params=pltpu.CompilerParams(
            collective_id=0, has_side_effects=True, vmem_limit_bytes=60 * 1024 * 1024
        ),
    )(estimate, measured, psf_z, psf_xy, offsets, coverage)


def solution(mesh):
    placed = (
        P(None, "tile", "view"),
        P("view", None, "tile", None),
        P("view", None),
        P("view", None, None),
        P("view", None),
        P("view", "tile"),
    )
    return jax.shard_map(
        body, mesh=mesh, in_specs=placed, out_specs=P(None, "tile", "view"), check_vma=False
    )
```

```python
import functools

import jax
import jax.numpy as jnp
from jax import lax
from jax.experimental import pallas as pl
from jax.experimental.pallas import tpu as pltpu
from jax.sharding import PartitionSpec as P

MESH = pl.DeviceIdType.MESH
F32, BF16 = jnp.float32, jnp.bfloat16
SHIFT, ITERS = 4, 2
NZ, TY, BX, NV, NT = 16, 32, 128, 8, 32
KZ, KXY = 65, 9
EXACT = lax.Precision.HIGHEST


def lanes(shape):
    return lax.broadcasted_iota(jnp.int32, shape, len(shape) - 1)


def toeplitz(row, count):
    x = jnp.broadcast_to(row, (count, row.shape[-1]))
    r = lax.broadcasted_iota(jnp.int32, x.shape, 0)
    bit = 1
    while bit < count:
        x = jnp.where((r & bit) != 0, pltpu.roll(x, bit, 1), x)
        bit *= 2
    return x


def kernel(
    est_hbm, meas, pz_hbm, pxy_hbm, offs_hbm, cov_hbm, out,
    est, pz, pxy, offs, cov,
    mbuf, pb, fld, hr, hl, sr, sl, mm, mq, mu, md, sq, su, sd, sx,
    rz, ry, az, ay, wf, wb, xf, xb, bl, mext, rt, acc, cur,
    loc, ps, pr, fs, fr, ms, mr, mx,
):
    v, t = lax.axis_index("view"), lax.axis_index("tile")
    has_up, has_down = t > 0, t < NT - 1
    has_left, has_right = v > 0, v < NV - 1

    def remote(src, dst, send, recv, dv, dt):
        return pltpu.make_async_remote_copy(
            src_ref=src, dst_ref=dst, send_sem=send, recv_sem=recv, device_id=(dv, dt), device_id_type=MESH
        )

    half, spot = v // 4, lax.rem(v, 4)

    def target_view(s):
        return lax.rem(half + s // 4, 2) * 4 + lax.rem(spot + s, 4)

    def source_view(s):
        return lax.rem(half + s // 4, 2) * 4 + lax.rem(spot + 8 - s, 4)

    odd = lax.rem(t, 2) == 1
    cross = lax.rem(t + NT - 1 + 2 * lax.rem(t, 2), NT)
    straight_down = t < 0
    straight_up = t < 0

    own_cols = pl.ds(pl.multiple_of(v * BX, BX), BX)
    get_all = pltpu.make_async_copy(meas.at[0], mbuf, loc.at[0])
    get_own = pltpu.make_async_copy(meas.at[0, :, :, own_cols], mm.at[v], loc.at[1])
    small = [
        pltpu.make_async_copy(src, dst, loc.at[2 + i])
        for i, (src, dst) in enumerate(
            ((pz_hbm, pz), (pxy_hbm, pxy), (offs_hbm, offs), (cov_hbm, cov), (est_hbm, est))
        )
    ]
    for copy in small:
        copy.start()
    get_all.start()
    get_own.start()

    barrier = pltpu.get_barrier_semaphore()
    up_tile, down_tile = lax.rem(t + NT - 1, NT), lax.rem(t + 1, NT)
    partners = [(lax.rem(v + s, NV), t) for s in range(1, NV)]
    partners += [(lax.rem(v + s, NV), dt) for s in (0, 1, NV - 1) for dt in (up_tile, down_tile)]
    for partner in partners:
        pl.semaphore_signal(barrier, inc=1, device_id=partner, device_id_type=MESH)
    for copy in small[:4]:
        copy.wait()

    lane1 = lanes((1, BX))
    zero1 = jnp.zeros((1, BX), F32)

    def taps(values, places):
        row = zero1
        for value, place in zip(values, places):
            row = jnp.where(lane1 == place, value, row)
        return row

    z_taps = [pz[0, i] for i in range(KZ)]
    y_taps = [pxy[0, 0, i] for i in range(KXY)]
    x_taps = [pxy[0, 1, i] for i in range(KXY)]
    oy, ox = offs[0, 0], offs[0, 1]

    def normal(values):
        return jnp.full((1, BX), functools.reduce(lambda a, b: a + b, values), F32)

    zn, yn, xn = normal(z_taps), normal(y_taps), normal(x_taps)
    rows = [
        taps(z_taps, range(KZ)) / zn,
        taps(z_taps, [KZ - 1 - i for i in range(KZ)]) / zn,
        taps(y_taps, [i + SHIFT + oy for i in range(KXY)]) / yn,
        taps(y_taps, [16 - (i + SHIFT + oy) for i in range(KXY)]) / yn,
        taps(x_taps, [4 - i - ox for i in range(KXY)]) / xn,
        taps(x_taps, [132 - i - ox for i in range(KXY)]) / xn,
        taps(x_taps, [i - 4 + ox for i in range(KXY)]) / xn,
        taps(x_taps, [i + 124 + ox for i in range(KXY)]) / xn,
        jnp.full((1, BX), cov[0, 0].astype(F32)),
    ]
    for i, row in enumerate(rows):
        pb[v, i : i + 1, :] = row
    pb[v, len(rows) :, :] = jnp.zeros((16 - len(rows), BX), F32)

    plane_lane = lanes((TY, BX))
    wide_lane = lanes((2 * TY, BX))

    def field_copies(it):
        f = fld.at[it]
        up, down, left, right = t - 1, t + 1, v - 1, v + 1
        top, low = pl.ds(0, 16), pl.ds(16, 16)
        main = pl.ds(0, BX)
        specs = [
            (has_up, has_down, f.at[:, pl.ds(16, 16), main], f.at[:, pl.ds(48, 16), main], v, up),
            (has_down, has_up, f.at[:, pl.ds(32, 16), main], f.at[:, pl.ds(0, 16), main], v, down),
        ]
        for ok_to, ok_from, s, h, dv in ((has_left, has_right, sr, hr, left), (has_right, has_left, sl, hl, right)):
            specs += [
                (ok_to, ok_from, s.at[it], h.at[it, :, pl.ds(16, 32)], dv, t),
                (ok_to & has_up, ok_from & has_down, s.at[it, :, top], h.at[it, :, pl.ds(48, 16)], dv, up),
                (ok_to & has_down, ok_from & has_up, s.at[it, :, low], h.at[it, :, pl.ds(0, 16)], dv, down),
            ]
        return [
            (ok_to, ok_from, dst, remote(src, dst, fs.at[it, i], fr.at[it, i], dv, dt))
            for i, (ok_to, ok_from, src, dst, dv, dt) in enumerate(specs)
        ]

    def pack_field(it, source):
        for z in range(NZ):
            fld[it, z, 16:48, 0:BX] = source[z].astype(BF16)

    def pack_sides(it, source):
        for q in range(2):
            head = jnp.zeros((TY, BX), F32)
            tail = jnp.zeros((TY, BX), F32)
            for k in range(8):
                rolled = source[8 * q + k]
                if k:
                    rolled = pltpu.roll(rolled, 16 * k, 1)
                head = jnp.where(plane_lane // 16 == k, rolled, head)
                tail = jnp.where(plane_lane // 16 == (k + 7) % 8, rolled, tail)
            sr[it, q] = head.astype(BF16)
            sl[it, q] = tail.astype(BF16)

    def send_field(it, which):
        for ok_to, _, _, copy in field_copies(it)[which]:
            pl.when(ok_to)(copy.start)

    rows, sides = slice(0, 2), slice(2, 8)

    def arrived(it, which):
        for _, ok_from, dst, copy in field_copies(it)[which]:
            pl.when(ok_from)(copy.wait_recv)

            @pl.when(jnp.logical_not(ok_from))
            def _():
                dst[...] = jnp.zeros(dst.shape, BF16)

    def receive_field(it):
        arrived(it, sides)
        for q in range(2):
            right = hr[it, q].astype(F32)
            left = hl[it, q].astype(F32)
            for k in range(8):
                both = jnp.where(wide_lane // 16 == k, right, left)
                if k:
                    both = pltpu.roll(both, BX - 16 * k, 1)
                both = jnp.where((wide_lane < 16) | (wide_lane >= 112), both, 0.0)
                fld[it, 8 * q + k, :, BX:] = both.astype(BF16)
        arrived(it, rows)

    small[4].wait()
    pack_field(0, est)
    pack_sides(0, est)
    get_all.wait()

    pl.semaphore_wait(barrier, len(partners))
    for s in range(1, NV):
        d = target_view(s)
        remote(pb.at[v], pb.at[v], ps.at[d], pr.at[v], d, t).start()
    send_field(0, slice(0, 8))
    for s in range(1, NV):
        d = target_view(s)
        cols = pl.ds(pl.multiple_of(d * BX, BX), BX)
        remote(mbuf.at[:, :, cols], mm.at[v], ms.at[0, d], mr.at[0, v], d, t).start()

    def straight_copies(d):
        return (
            (straight_down, remote(sx.at[d], mu.at[v], mx.at[d], mr.at[2, v], d, t + 1)),
            (straight_up, remote(sx.at[d], md.at[v], mx.at[d], mr.at[3, v], d, t - 1)),
        )

    def pack_columns(s, carry):
        d = target_view(s)
        after = pl.ds(pl.multiple_of(jnp.minimum(d + 1, NV - 1) * BX, BX), BX)
        before = pl.ds(pl.multiple_of(jnp.maximum(d - 1, 0) * BX, BX), BX)
        take_after = (plane_lane < 8) & (d < NV - 1)
        take_before = (plane_lane >= 120) & (d > 0)
        corner = []
        for q in range(2):
            packed = jnp.zeros((TY, BX), F32)
            for k in range(8):
                z = 8 * q + k
                edge = jnp.where(
                    take_after, mbuf[z, :, after].astype(F32),
                    jnp.where(take_before, mbuf[z, :, before].astype(F32), 0.0),
                )
                packed = packed + (pltpu.roll(edge, 16 * k, 1) if k else edge)
            corner.append(packed)
            sq[d, q] = packed.astype(BF16)

        @pl.when(s > 0)
        def _():
            remote(sq.at[d], mq.at[v], ms.at[1, d], mr.at[1, v], d, t).start()

        @pl.when((s >= 4) & (straight_up | straight_down))
        def _():
            here = pl.ds(pl.multiple_of(d * BX, BX), BX)

            def edge_rows(a):
                return jnp.where(odd, a[24:32], a[0:8])

            for p in range(9):
                if p < 8:
                    a, b = mbuf[2 * p, :, here].astype(F32), mbuf[2 * p + 1, :, here].astype(F32)
                else:
                    a, b = corner
                sx[d, p] = jnp.concatenate([edge_rows(a), edge_rows(b)], axis=0).astype(BF16)
            for ok_to, copy in straight_copies(d):
                pl.when(ok_to)(copy.start)

        return carry

    lax.fori_loop(0, NV, pack_columns, 0)
    mq[v] = sq[v]

    for s in range(1, NV):
        u = lax.rem(v + s, NV)
        remote(pb.at[u], pb.at[u], ps.at[u], pr.at[u], u, t).wait_recv()

    def small_bands(u, carry):
        z16 = pl.ds(pl.multiple_of(u * 16, 16), 16)
        for half in range(2):
            rz[half, z16, :] = toeplitz(pb[u, half : half + 1, :], 16)
            ry[half, z16, :] = toeplitz(pb[u, 2 + half : 3 + half, :], 16)
        for source, target in ((4, xf), (6, xb)):
            row = jnp.concatenate([pb[u, source : source + 1, :], pb[u, source + 1 : source + 2, :]], axis=1)
            base = toeplitz(row, 16)
            width = target.shape[-1]
            for g in range(16):
                part = (pltpu.roll(base, 16 * g, 1) if g else base)[:, :width]
                target[u, 16 * g : 16 * g + 16, :] = part.astype(BF16)
        return carry

    lax.fori_loop(0, NV, small_bands, 0)
    m = lax.broadcasted_iota(jnp.int32, (BX, 512), 0)
    n = lanes((BX, 512))
    spread_z = (m == n // 32 + 32).astype(F32)
    spread_y = (m == n % 32).astype(F32)
    for way in range(2):
        az[way] = jnp.dot(rz[way], spread_z, precision=EXACT, preferred_element_type=F32)
        ay[way] = jnp.dot(ry[way], spread_y, precision=EXACT, preferred_element_type=F32)

    def depth_rows(u, carry):
        z16 = pl.ds(pl.multiple_of(u * 16, 16), 16)
        for half, target in enumerate((wf, wb)):
            a = az[half, z16, :]
            y = ay[half, z16, :]
            for z in range(NZ):
                target[u, 16 * z : 16 * z + 16, :] = (a[z : z + 1] * y).astype(BF16)
        return carry

    lax.fori_loop(0, NV, depth_rows, 0)

    def blur(it, u):
        parts = []
        for c in range(3):
            chunk = fld[it, :, 16 * c : 16 * c + 32, :].reshape(512, 256)
            parts.append(jnp.dot(wf[u], chunk, preferred_element_type=F32).astype(BF16))
        return jnp.dot(jnp.concatenate(parts, axis=0), xf[u], preferred_element_type=F32)

    def relay_copies(u):
        far = u // 4 != half
        skip_down = far & (t < 0)
        skip_up = far & (t < 0)
        return (
            (has_down & jnp.logical_not(skip_down), has_up, remote(su.at[u], mu.at[u], ms.at[2, u], mr.at[2, u], v, t + 1)),
            (has_up & jnp.logical_not(skip_up), has_down, remote(sd.at[u], md.at[u], ms.at[3, u], mr.at[3, u], v, t - 1)),
        )

    def relay(u):
        @pl.when(u != v)
        def _():
            remote(mbuf.at[:, :, pl.ds(0, BX)], mm.at[u], ms.at[0, u], mr.at[0, u], u, t).wait_recv()
            remote(sq.at[u], mq.at[u], ms.at[1, u], mr.at[1, u], u, t).wait_recv()

        for p in range(9):
            if p < 8:
                a, b = mm[u, 2 * p].astype(F32), mm[u, 2 * p + 1].astype(F32)
            else:
                a, b = mq[u, 0].astype(F32), mq[u, 1].astype(F32)
            sd[u, p] = jnp.concatenate([a[0:8], b[0:8]], axis=0).astype(BF16)
            su[u, p] = jnp.concatenate([a[24:32], b[24:32]], axis=0).astype(BF16)
        for ok_to, _, copy in relay_copies(u):
            pl.when(ok_to)(copy.start)

    ext_lane = lanes((48, BX))

    @pl.when(jnp.logical_not(has_up))
    def _():
        mu[...] = jnp.zeros(mu.shape, BF16)

    @pl.when(jnp.logical_not(has_down))
    def _():
        md[...] = jnp.zeros(md.shape, BF16)

    def ratio(values, blurred):
        return jnp.where(values > 0, values / blurred, 0.0).astype(BF16)

    def assemble(u):
        cu, cd = mu[u, 8].astype(F32), md[u, 8].astype(F32)
        for q in range(2):
            rows8 = slice(8 * q, 8 * q + 8)
            edge = jnp.concatenate([cu[rows8], mq[u, q].astype(F32), cd[rows8]], axis=0)
            for k in range(8):
                z = 8 * q + k
                side = pltpu.roll(edge, BX - 16 * k, 1) if k else edge
                side = jnp.where((ext_lane < 8) | (ext_lane >= 120), side, 0.0)
                mext[u, z, :, BX:] = side.astype(BF16)
                rt[z, :, BX:] = ratio(side, bl[u, z, :, BX:])
                r = slice(8 * (z % 2), 8 * (z % 2) + 8)
                main = jnp.concatenate(
                    [mu[u, z // 2].astype(F32)[r], mm[u, z].astype(F32), md[u, z // 2].astype(F32)[r]], axis=0
                )
                mext[u, z, :, :BX] = main.astype(BF16)
                rt[z, :, :BX] = ratio(main, bl[u, z, :, :BX])

    def correct(u, ratios):
        weight = pb[u, 8:9, :]
        rows = jnp.dot(ratios.reshape(768, 256), xb[u], preferred_element_type=F32).astype(BF16)
        rows = rows.reshape(NZ, 48, BX)
        chunks = jnp.concatenate([rows[:, 0:32].reshape(512, BX), rows[:, 16:48].reshape(512, BX)], axis=1)
        back = jnp.dot(wb[u], chunks, preferred_element_type=F32)
        for c in range(2):
            log_back = weight * jnp.log(back[:, BX * c : BX * c + BX])
            acc[:, 16 * c : 16 * c + 16, :] += log_back.reshape(NZ, 16, BX)

    count = pb[0, 8:9, :]
    for u in range(1, NV):
        count = count + pb[u, 8:9, :]

    get_own.wait()

    def relay_step(s, carry):
        relay(source_view(s))
        return carry

    receive_field(0)
    acc[...] = jnp.zeros(acc.shape, F32)

    def first_forward(s, carry):
        u = source_view(s)
        full = blur(0, u)
        for c in range(3):
            bl[u, :, 16 * c : 16 * c + 16, :] = full[256 * c : 256 * c + 256].reshape(NZ, 16, 256)
        return carry

    lax.fori_loop(0, 4, first_forward, 0, unroll=4)
    lax.fori_loop(0, 4, relay_step, 0)
    lax.fori_loop(4, NV, first_forward, 0, unroll=4)

    def first_backward(s, carry):
        u = source_view(s)
        for _, ok_from, copy in relay_copies(u):
            pl.when(ok_from)(copy.wait_recv)
        assemble(u)
        correct(u, rt[...])
        return carry

    lax.fori_loop(4, NV, relay_step, 0)
    lax.fori_loop(0, NV, first_backward, 0, unroll=4)
    for z in range(NZ):
        cur[z] = est[z] * jnp.exp(acc[z] / count)
    pack_field(1, cur)
    send_field(1, rows)
    pack_sides(1, cur)
    send_field(1, sides)
    acc[...] = jnp.zeros(acc.shape, F32)

    def drain(s, carry):
        d = lax.rem(v + s, NV)

        @pl.when(d != v)
        def _():
            remote(pb.at[v], pb.at[v], ps.at[d], pr.at[d], d, t).wait_send()
            remote(mbuf.at[:, :, pl.ds(0, BX)], mm.at[v], ms.at[0, d], mr.at[0, d], d, t).wait_send()
            remote(sq.at[d], mq.at[v], ms.at[1, d], mr.at[1, d], d, t).wait_send()

        for ok_to, _, copy in relay_copies(d):
            pl.when(ok_to)(copy.wait_send)
        for ok_to, copy in straight_copies(d):
            pl.when(ok_to & (d // 4 != half))(copy.wait_send)
        return carry

    lax.fori_loop(0, NV, drain, 0)

    receive_field(1)

    def second(u, carry):
        full = blur(1, u)
        for c in range(3):
            part = full[256 * c : 256 * c + 256].reshape(NZ, 16, 256)
            rt[:, 16 * c : 16 * c + 16, :] = ratio(mext[u, :, 16 * c : 16 * c + 16, :].astype(F32), part)
        correct(u, rt[...])
        return carry

    lax.fori_loop(0, NV, second, 0, unroll=8)
    for z in range(NZ):
        out[z] = cur[z] * jnp.exp(acc[z] / count)

    for it in range(ITERS):
        for ok_to, _, _, copy in field_copies(it):
            pl.when(ok_to)(copy.wait_send)


def body(estimate, measured, psf_z, psf_xy, offsets, coverage):
    scratch = [
        ((NZ, TY, NV * BX), BF16), ((NV, 16, BX), F32),
        ((2, NZ, 64, 256), BF16), ((2, 2, 64, BX), BF16), ((2, 2, 64, BX), BF16),
        ((2, 2, TY, BX), BF16), ((2, 2, TY, BX), BF16),
        ((NV, NZ, TY, BX), BF16), ((NV, 2, TY, BX), BF16), ((NV, 9, 16, BX), BF16), ((NV, 9, 16, BX), BF16),
        ((NV, 2, TY, BX), BF16), ((NV, 9, 16, BX), BF16), ((NV, 9, 16, BX), BF16), ((NV, 9, 16, BX), BF16),
        ((2, 128, BX), F32), ((2, 128, BX), F32), ((2, 128, 512), F32), ((2, 128, 512), F32),
        ((NV, 256, 512), BF16), ((NV, 256, 512), BF16), ((NV, 256, 256), BF16), ((NV, 256, BX), BF16),
        ((NV, NZ, 48, 256), F32), ((NV, NZ, 48, 256), BF16), ((NZ, 48, 256), BF16), ((NZ, TY, BX), F32), ((NZ, TY, BX), F32),
    ]
    dma = pltpu.SemaphoreType.DMA
    return pl.pallas_call(
        kernel,
        out_shape=jax.ShapeDtypeStruct(estimate.shape, F32),
        in_specs=[pl.BlockSpec(memory_space=pl.ANY)] * 6,
        out_specs=pl.BlockSpec(memory_space=pltpu.VMEM),
        scratch_shapes=[
            pltpu.VMEM((NZ, TY, BX), F32),
            pltpu.SMEM((1, KZ), F32),
            pltpu.SMEM((1, 2, KXY), F32),
            pltpu.SMEM((1, 2), jnp.int32),
            pltpu.SMEM((1, 1), jnp.int32),
        ]
        + [pltpu.VMEM(s, d) for s, d in scratch]
        + [dma((7,)), dma((NV,)), dma((NV,)), dma((2, 8)), dma((2, 8)), dma((4, NV)), dma((4, NV)), dma((NV,))],
        compiler_params=pltpu.CompilerParams(
            collective_id=0, has_side_effects=True, vmem_limit_bytes=60 * 1024 * 1024
        ),
    )(estimate, measured, psf_z, psf_xy, offsets, coverage)


def solution(mesh):
    placed = (
        P(None, "tile", "view"),
        P("view", None, "tile", None),
        P("view", None),
        P("view", None, None),
        P("view", None),
        P("view", "tile"),
    )
    return jax.shard_map(
        body, mesh=mesh, in_specs=placed, out_specs=P(None, "tile", "view"), check_vma=False
    )
```
